128 devices in a mesh: section: 16 (over y, x_lo, core), peer: 8 (over x_hi, z).
Axes of the slice: x: 4 (x_hi: 2, x_lo: 2; x = x_hi * 2 + x_lo), y: 4, z: 4, core: 2. Of those that a mesh axis runs over, the one named last changes fastest.
Arguments:
- inputs: bfloat16 [16, 8, 128, 2560], P('section', 'peer'), may hold values from -6 to 6
- wiring: int32 [2, 16, 8], replicated, may hold values from 0 to 7, as said below
- lengths: int32 [16, 8], replicated, may hold values from 16 to 128
- norm_gain: bfloat16 [16, 2560], P('section'), may hold values from 0.25 to 1.75
- w_query: bfloat16 [16, 2560, 3072], P('section', None, 'peer'), may hold values from -0.5 to 0.5
- w_key: bfloat16 [16, 2560, 3072], P('section', None, 'peer'), may hold values from -0.5 to 0.5
- w_value: bfloat16 [16, 2560, 3072], P('section', None, 'peer'), may hold values from -0.125 to 0.125
- w_out: bfloat16 [16, 3072, 2560], P('section', 'peer'), may hold values from -0.109375 to 0.109375
- cotangent: bfloat16 [16, 8, 128, 2560], P('section', 'peer'), may hold values from -0.59765625 to 0.59765625
Outputs:
- final_out: bfloat16 [16, 8, 128, 2560], P('section', 'peer')
- input_grad: bfloat16 [16, 8, 128, 2560], P('section', 'peer')
- gain_grad: float32 [16, 2560], P('section')
- w_query_grad: bfloat16 [16, 2560, 3072], P('section', None, 'peer')
- w_key_grad: bfloat16 [16, 2560, 3072], P('section', None, 'peer')
- w_value_grad: bfloat16 [16, 2560, 3072], P('section', None, 'peer')
- w_out_grad: bfloat16 [16, 3072, 2560], P('section', 'peer')
The draws below stay inside these ranges and needn't reach their ends.
Inputs may be any that keep to these rules, and one draw needn't show every extreme that they name: Each wiring[h, s, :] is a permutation of the peers 0 to 7.
All inputs are finite; a program needn't handle non-finite values.
Results may differ from the reference program's by a relative error of at most 0.022.
The reference program's roundings to bfloat16 on the way (of `entering`, `normed`, `query_heads`, `mixed`, `layer_out`, `d_scores` and `d_query`) count: a program that leaves them out, or rounds other values in their place, can miss the bound.
Values may be sent and summed in bfloat16 or wider, within the bound.
No kernel may reach another device: no remote copies, remote signals or barrier semaphores. Data moves between devices by JAX's collectives and lax.ppermute only.
A program may use at most 192 MiB of HBM per device.

```python
import math
import jax
import jax.numpy as jnp
from jax import lax

D = 2560
HD = 128
TOK = 128
INNER = 3072
SECTIONS = 16
PEERS = 8


def shared_base(key):
    return jax.random.normal(key, (SECTIONS, D, INNER), jnp.float32)


def draw_w_query(key, part):
    base = shared_base(key)
    weight_scale = D ** (-0.5)
    values = base * weight_scale
    return jnp.clip(values, -0.5, 0.5).astype(jnp.bfloat16)


def draw_w_key(key, part):
    key = jax.random.fold_in(key, 37)
    weight_scale = D ** (-0.5)
    own = jax.random.normal(key, (SECTIONS, D, INNER), jnp.float32)
    values = own * weight_scale
    return jnp.clip(values, -0.5, 0.5).astype(jnp.bfloat16)


def draw_inputs(key, part):
    key = jax.random.fold_in(key, 41)
    shape = (SECTIONS, PEERS, TOK, D)
    values = jax.random.normal(key, shape, jnp.float32)
    return jnp.clip(values, -6.0, 6.0).astype(jnp.bfloat16)


def draw_wiring(key, part):
    key = jax.random.fold_in(key, 11)
    row_keys = jax.random.split(key, 2 * SECTIONS)
    perms = jax.vmap(lambda one_key: jax.random.permutation(one_key, PEERS))(row_keys)
    return perms.reshape(2, SECTIONS, PEERS).astype(jnp.int32)


def draw_lengths(key, part):
    key = jax.random.fold_in(key, 23)
    base_key, high_key, low_key = jax.random.split(key, 3)
    total = SECTIONS * PEERS
    base = jax.random.randint(base_key, (total,), TOK // 8, TOK + 1, dtype=jnp.int32)
    high_pos = jax.random.randint(high_key, (), 0, total, dtype=jnp.int32)
    low_pos = (high_pos + 1 + jax.random.randint(low_key, (), 0, total - 1, dtype=jnp.int32)) % total
    positions = jnp.arange(total, dtype=jnp.int32)
    base = jnp.where(positions == high_pos, TOK, base)
    base = jnp.where(positions == low_pos, TOK // 8, base)
    return base.reshape(SECTIONS, PEERS).astype(jnp.int32)


def steps_of(key, extent, shards, low, high):
    factor_of, own = 1.0, jax.random.fold_in(key, 6)
    for dim, parts in shards:
        heights = jnp.exp(jax.random.uniform(jax.random.fold_in(own, dim), (parts,), jnp.float32, low / len(shards), high / len(shards)))
        factor_of = factor_of * jnp.repeat(heights, extent[dim] // parts).reshape([-1 if axis == dim else 1 for axis in range(len(extent))])
    return factor_of


def centred(rng, dims, deviation, reach, cuts=(), held_as=jnp.bfloat16):
    array = jax.random.normal(rng, dims, jnp.float32) * deviation
    if len(cuts) > 0:
        array = steps_of(rng, dims, cuts, -0.22, 0.18) * array
    return jnp.clip(array, min=-reach, max=reach).astype(held_as)


def setup_inputs(seed: int = 0) -> dict:
    splits = jax.random.split(jax.random.key(seed), 10)
    inputs = draw_inputs(jax.random.fold_in(splits[9], 71), 0)
    wiring = draw_wiring(jax.random.fold_in(splits[9], 71), 0)
    lengths = draw_lengths(jax.random.fold_in(splits[9], 71), 0)
    norm_gain = jnp.clip(1.0 + 0.15 * jax.random.normal(splits[3], (SECTIONS, D), jnp.float32), 0.25, 1.75).astype(jnp.bfloat16)
    w_query = draw_w_query(jax.random.fold_in(splits[9], 71), 0)
    w_key = draw_w_key(jax.random.fold_in(splits[9], 71), 0)
    w_value = centred(splits[6], (SECTIONS, D, INNER), D ** -0.5, 0.125, ((0, 16), (2, 8)))
    w_out = centred(splits[7], (SECTIONS, INNER, D), INNER ** -0.5, 0.109375, ((0, 16), (1, 8)))
    cotangent = centred(splits[8], (SECTIONS, PEERS, TOK, D), 0.1, 0.59765625, ((0, 16), (1, 8)))
    return {"inputs": inputs, "wiring": wiring, "lengths": lengths, "norm_gain": norm_gain, "w_query": w_query, "w_key": w_key, "w_value": w_value, "w_out": w_out, "cotangent": cotangent}


eps = 1e-05

def invert(permutation):
    peer_count = permutation.shape[-1]
    numbers = jnp.arange(peer_count, dtype=jnp.int32)
    matches = permutation[..., None, :] == numbers[:, None]
    return lax.optimization_barrier(jnp.sum(jnp.where(matches, numbers, 0), axis=-1)).astype(jnp.int32)

def lookup(table_rows, positions):
    peer_count = table_rows.shape[-1]
    numbers = jnp.arange(peer_count, dtype=jnp.int32)
    matches = positions[..., :, None] == numbers
    return lax.optimization_barrier(jnp.sum(jnp.where(matches, table_rows[..., None, :], 0), axis=-1)).astype(jnp.int32)

def probabilities(query_heads, key_heads, seq_lengths):
    seq_rows = query_heads.shape[1]
    score_scale = 1.0 / math.sqrt(query_heads.shape[3])
    scores = jnp.einsum('mihc,mjhc->mhij', query_heads.astype(jnp.float32), key_heads.astype(jnp.float32)) * score_scale
    positions = jnp.arange(seq_rows, dtype=jnp.int32)
    allowed = (positions[None, :, None] >= positions[None, None, :]) & (positions[None, None, :] < seq_lengths[:, None, None])
    scores = jnp.where(allowed[:, None], scores, -1e+30)
    row_max = lax.optimization_barrier(jnp.max(scores, axis=-1, keepdims=True))
    exp_scores = jnp.exp(scores - row_max)
    return exp_scores / lax.optimization_barrier(jnp.sum(exp_scores, axis=-1, keepdims=True))

def section_pass(entering, seq_lengths, d_out, norm_gain, w_query, w_key, w_value, w_out):
    batches, seq_rows, model_width = entering.shape
    all_heads = w_query.shape[1] // HD
    score_scale = 1.0 / math.sqrt(HD)
    act_full = entering.astype(jnp.float32)
    inv_rms = lax.rsqrt(lax.optimization_barrier(jnp.mean(act_full * act_full, axis=-1, keepdims=True)) + eps)
    unit_rows = act_full * inv_rms
    gain_full = norm_gain.astype(jnp.float32)
    normed = (unit_rows * gain_full).astype(jnp.bfloat16).reshape(batches * seq_rows, model_width)

    def project(weight_mat):
        product = jnp.dot(normed, weight_mat, preferred_element_type=jnp.float32)
        return product.astype(jnp.bfloat16).reshape(batches, seq_rows, all_heads, HD)
    query_heads = project(w_query)
    key_heads = project(w_key)
    value_heads = project(w_value)
    attn_probs = probabilities(query_heads, key_heads, seq_lengths)
    probs_low = attn_probs.astype(jnp.bfloat16)
    mixed = jnp.einsum('mhij,mjhc->mihc', probs_low.astype(jnp.float32), value_heads.astype(jnp.float32))
    mixed = mixed.astype(jnp.bfloat16).reshape(batches * seq_rows, all_heads * HD)
    projected = jnp.dot(mixed, w_out, preferred_element_type=jnp.float32).reshape(batches, seq_rows, model_width)
    layer_out = (act_full + projected).astype(jnp.bfloat16)
    grad_rows = d_out.reshape(batches * seq_rows, model_width)
    d_mixed = jnp.dot(grad_rows, w_out.T, preferred_element_type=jnp.float32).astype(jnp.bfloat16)
    w_out_grad = jnp.dot(mixed.T, grad_rows, preferred_element_type=jnp.float32).astype(jnp.bfloat16)
    d_mixed = d_mixed.reshape(batches, seq_rows, all_heads, HD)
    d_values = jnp.einsum('mhij,mihc->mjhc', probs_low.astype(jnp.float32), d_mixed.astype(jnp.float32)).astype(jnp.bfloat16)
    d_probs = jnp.einsum('mihc,mjhc->mhij', d_mixed.astype(jnp.float32), value_heads.astype(jnp.float32))
    row_delta = lax.optimization_barrier(jnp.sum(attn_probs * d_probs, axis=-1, keepdims=True))
    d_scores = (attn_probs * (d_probs - row_delta) * score_scale).astype(jnp.bfloat16)
    d_query = jnp.einsum('mhij,mjhc->mihc', d_scores.astype(jnp.float32), key_heads.astype(jnp.float32)).astype(jnp.bfloat16)
    d_keys = jnp.einsum('mhij,mihc->mjhc', d_scores.astype(jnp.float32), query_heads.astype(jnp.float32)).astype(jnp.bfloat16)
    flat_q = d_query.reshape(batches * seq_rows, all_heads * HD)
    flat_k = d_keys.reshape(batches * seq_rows, all_heads * HD)
    flat_v = d_values.reshape(batches * seq_rows, all_heads * HD)
    w_query_grad = jnp.dot(normed.T, flat_q, preferred_element_type=jnp.float32).astype(jnp.bfloat16)
    w_key_grad = jnp.dot(normed.T, flat_k, preferred_element_type=jnp.float32).astype(jnp.bfloat16)
    w_value_grad = jnp.dot(normed.T, flat_v, preferred_element_type=jnp.float32).astype(jnp.bfloat16)
    d_normed = jnp.dot(flat_q, w_query.T, preferred_element_type=jnp.float32)
    d_normed = d_normed + jnp.dot(flat_k, w_key.T, preferred_element_type=jnp.float32)
    d_normed = d_normed + jnp.dot(flat_v, w_value.T, preferred_element_type=jnp.float32)
    d_normed = d_normed.reshape(batches, seq_rows, model_width)
    gain_grad = lax.optimization_barrier(jnp.sum(d_normed * unit_rows, axis=(0, 1)))
    scaled = d_normed * gain_full
    d_act = inv_rms * (scaled - unit_rows * lax.optimization_barrier(jnp.mean(scaled * unit_rows, axis=-1, keepdims=True)))
    d_entering = (d_out.astype(jnp.float32) + d_act).astype(jnp.bfloat16)
    return (layer_out, d_entering, gain_grad, w_query_grad, w_key_grad, w_value_grad, w_out_grad)

def reference(inputs, wiring, lengths, norm_gain, w_query, w_key, w_value, w_out, cotangent):
    entering = jnp.roll(inputs, 1, axis=0)
    lens_in = jnp.roll(lengths, 1, axis=0)
    first_map = jnp.roll(wiring[0], 1, axis=0)
    onward = lookup(wiring[1], first_map)
    later = jnp.roll(cotangent, -1, axis=0)
    d_out = jnp.take_along_axis(later, onward[:, :, None, None], axis=1)

    def one_section(packed):
        return section_pass(*packed)
    results = lax.map(one_section, (entering, lens_in, d_out, norm_gain, w_query, w_key, w_value, w_out))
    layer_out, d_entering, gain_grad, w_query_grad, w_key_grad, w_value_grad, w_out_grad = results
    placed = jnp.take_along_axis(layer_out, invert(onward)[:, :, None, None], axis=1)
    final_out = jnp.roll(placed, 1, axis=0)
    input_grad = jnp.roll(d_entering, -1, axis=0)
    return (final_out, input_grad, gain_grad, w_query_grad, w_key_grad, w_value_grad, w_out_grad)
```

```python
import functools
import math

import jax
import jax.numpy as jnp
from jax import lax
from jax.experimental import pallas as pl
from jax.experimental.pallas import tpu as pltpu
from jax.sharding import PartitionSpec as P

HD = 128
TOK = 128
HALF = TOK // 2
HEADS = 3
LOCAL = HEADS * HD
D = 2560
SECTIONS = 16
RING = 4
SCALE = 1.0 / math.sqrt(HD)
eps = 1e-05

F32 = jnp.float32
BF16 = jnp.bfloat16
VMEM_LIMIT = 48 * 1024 * 1024


def moved(value, by_section, flip, by_ring):
    pairs = []
    for section in range(SECTIONS):
        for side in range(2):
            for place in range(RING):
                source = (section * 2 + side) * RING + place
                target = ((section + by_section) % SECTIONS * 2 + (side ^ flip)) * RING
                pairs.append((source, target + (place + by_ring) % RING))
    return lax.ppermute(value, ("section", "peer"), pairs)


def gather_all(own, by):
    held = {}
    held[0] = moved(own, by, 0, 0)
    held[1] = moved(own, by, 1, 0)
    held[6] = moved(own, by, 0, 1)
    held[2] = moved(own, by, 0, -1)
    held[7] = moved(held[1], 0, 0, 1)
    held[3] = moved(held[1], 0, 0, -1)
    parts = [(held[r], 0, r) for r in (0, 1, 2, 6, 3, 7)]
    for dx in range(2):
        parts.append((moved(held[6 + dx][:HALF], 0, 0, 1), 0, 4 + dx))
        parts.append((moved(held[2 + dx][HALF:], 0, 0, -1), HALF, 4 + dx))
    return parts


WHERE = [(0, 0, TOK), (1, 0, TOK), (2, 0, TOK), (6, 0, TOK), (3, 0, TOK), (7, 0, TOK)] + [
    (4, 0, HALF),
    (4, HALF, HALF),
    (5, 0, HALF),
    (5, HALF, HALF),
]


def nt(a, b):
    return lax.dot_general(a, b, (((1,), (1,)), ((), ())), preferred_element_type=F32)


def tn(a, b):
    return lax.dot_general(a, b, (((0,), (0,)), ((), ())), preferred_element_type=F32)


def nn(a, b):
    return jnp.dot(a, b, preferred_element_type=F32)


def load_all(refs, target, sems):
    copies = []
    for k, (number, row, rows) in enumerate(WHERE):
        copies.append(
            pltpu.make_async_copy(refs[k], target.at[number, pl.ds(row, rows)], sems.at[k])
        )
    for copy in copies:
        copy.start()
    for copy in copies:
        copy.wait()


def load_one(refs, wanted, target, sems):
    for k, (number, row, rows) in enumerate(WHERE):

        @pl.when(wanted == number)
        def _(k=k, row=row, rows=rows):
            copy = pltpu.make_async_copy(refs[k], target.at[pl.ds(row, rows)], sems.at[k])
            copy.start()
            copy.wait()


def forward_kernel(
    ids, wiring, lengths, gain, wq, wk, wv, *rest
):
    parts = rest[:10]
    sigma, normed, qkv, probs, mixed, entering, sems = rest[10:]
    section, side, place = ids[0], ids[1], ids[2]
    before = lax.rem(section + SECTIONS - 1, SECTIONS)

    def absolute(r):
        dz, dx = r // 2, r % 2
        return lax.rem(side + dx, 2) * RING + lax.rem(place + dz, RING)

    for r in range(8):
        slot = absolute(r)
        found = jnp.int32(0)
        for m in range(8):
            goes_to = wiring[1, section, wiring[0, before, absolute(m)]]
            found = found + jnp.where(goes_to == slot, m, 0)
        sigma[r] = found

    load_all(parts, entering, sems)
    gain_row = gain[...].astype(F32)

    def norm_one(r, carry):
        act = entering[r].astype(F32)
        inv_rms = lax.rsqrt(jnp.mean(act * act, axis=-1, keepdims=True) + eps)
        normed[r] = (act * inv_rms * gain_row).astype(BF16)
        return carry

    lax.fori_loop(0, 8, norm_one, 0)

    def project(j, carry):
        rows = normed[pl.ds(2 * j, 2)].reshape(2 * TOK, D)
        for c, w in enumerate((wq, wk, wv)):
            out = nn(rows, w[0]).astype(BF16).reshape(2, TOK, LOCAL)
            qkv[pl.ds(2 * j, 2), :, c * LOCAL : (c + 1) * LOCAL] = out
        return carry

    lax.fori_loop(0, 4, project, 0)

    row = lax.broadcasted_iota(jnp.int32, (TOK, TOK), 0)
    col = lax.broadcasted_iota(jnp.int32, (TOK, TOK), 1)

    def attend(r, carry):
        seq_len = lengths[before, absolute(r)]
        allowed = (row >= col) & (col < seq_len)
        for h in range(HEADS):
            q = qkv[r, :, h * HD : (h + 1) * HD]
            k = qkv[r, :, LOCAL + h * HD : LOCAL + (h + 1) * HD]
            v = qkv[r, :, 2 * LOCAL + h * HD : 2 * LOCAL + (h + 1) * HD]
            scores = jnp.where(allowed, nt(q, k) * SCALE, -1e30)
            exp_scores = jnp.exp(scores - jnp.max(scores, axis=-1, keepdims=True))
            p = exp_scores / jnp.sum(exp_scores, axis=-1, keepdims=True)
            probs[r, h] = p
            mixed[r, :, h * HD : (h + 1) * HD] = nn(p.astype(BF16), v).astype(BF16)
        return carry

    lax.fori_loop(0, 8, attend, 0)


ANY = pl.BlockSpec(memory_space=pl.ANY)
SMEM = pl.BlockSpec(memory_space=pltpu.SMEM)
VMEM = pl.BlockSpec(memory_space=pltpu.VMEM)


def params(**more):
    return pltpu.CompilerParams(vmem_limit_bytes=VMEM_LIMIT, **more)


def cost(flops, moved_bytes):
    return pl.CostEstimate(flops=int(flops), bytes_accessed=int(moved_bytes), transcendentals=0)


def forward(ids, wiring, lengths, gain, wq, wk, wv, parts):
    return pl.pallas_call(
        forward_kernel,
        out_shape=(
            jax.ShapeDtypeStruct((8,), jnp.int32),
            jax.ShapeDtypeStruct((8, TOK, D), BF16),
            jax.ShapeDtypeStruct((8, TOK, 3 * LOCAL), BF16),
            jax.ShapeDtypeStruct((8, HEADS, TOK, TOK), F32),
            jax.ShapeDtypeStruct((8, TOK, LOCAL), BF16),
        ),
        in_specs=[SMEM] * 3 + [VMEM] * 4 + [ANY] * 10,
        out_specs=(SMEM, VMEM, VMEM, VMEM, VMEM),
        scratch_shapes=[pltpu.VMEM((8, TOK, D), BF16), pltpu.SemaphoreType.DMA((10,))],
        compiler_params=params(),
        cost_estimate=cost(6.3e9, 20e6),
        name="forward",
    )(ids, wiring, lengths, gain, wq, wk, wv, *parts)


PIECES = {
    "u_up": (4, 0, HALF),
    "u_down": (4, HALF, HALF),
    "v_up": (2, HALF, HALF),
    "v_down": (6, 0, HALF),
    "k_up": (2, 0, HALF),
    "k_down": (6, HALF, HALF),
    "own": (0, 0, TOK),
}
TILE = 512


def store_pieces(outs, total):
    for out, (number, row, rows) in zip(outs, PIECES.values(), strict=True):
        out[...] = total[number : number + 2, row : row + rows].astype(BF16)


def piece_shapes():
    return tuple(jax.ShapeDtypeStruct((2, rows, D), BF16) for _, _, rows in PIECES.values())


def piece_specs():
    return tuple(pl.BlockSpec((2, rows, TILE), lambda n: (0, 0, n)) for _, _, rows in PIECES.values())


def outward_kernel(sigma, mixed, wo, *rest):
    parts = rest[:10]
    outs = rest[10:17]
    sent = rest[17]
    entering, sems = rest[18:]
    tile = pl.program_id(0)

    @pl.when(tile == 0)
    def _():
        for r in range(8):
            sent[r] = mixed[sigma[r]]
        load_one(parts, sigma[0], entering, sems)

    total = nn(sent[...].reshape(8 * TOK, LOCAL), wo[0]).reshape(8, TOK, TILE)
    for out, (number, row, rows) in zip(outs[:6], list(PIECES.values())[:6], strict=True):
        out[...] = total[number : number + 2, row : row + rows].astype(BF16)
    residual = entering[:, pl.ds(pl.multiple_of(tile * TILE, TILE), TILE)].astype(F32)
    outs[6][0] = (total[0] + residual).astype(BF16)
    outs[6][1] = total[1].astype(BF16)


def outward(sigma, mixed, wo, parts):
    whole = lambda *shape: pl.BlockSpec(shape, lambda n: (0,) * len(shape))
    return pl.pallas_call(
        outward_kernel,
        grid=(D // TILE,),
        out_shape=piece_shapes() + (jax.ShapeDtypeStruct((8, TOK, LOCAL), BF16),),
        in_specs=[SMEM, whole(8, TOK, LOCAL), pl.BlockSpec((1, LOCAL, TILE), lambda n: (0, 0, n))]
        + [ANY] * 10,
        out_specs=piece_specs() + (whole(8, TOK, LOCAL),),
        scratch_shapes=[pltpu.VMEM((TOK, D), BF16), pltpu.SemaphoreType.DMA((10,))],
        compiler_params=params(),
        cost_estimate=cost(2e9, 9e6),
        name="outward",
    )(sigma, mixed, wo, *parts)


def back_kernel(sigma, wo, qkv, probs, *rest):
    parts = rest[:10]
    dqkv, grads, d_mixed, sems = rest[10:]
    load_all(parts, grads, sems)

    def project(j, carry):
        rows = grads[pl.ds(2 * j, 2)].reshape(2 * TOK, D)
        d_mixed[pl.ds(2 * j, 2)] = nt(rows, wo[0]).astype(BF16).reshape(2, TOK, LOCAL)
        return carry

    lax.fori_loop(0, 4, project, 0)

    def attend(r, carry):
        m = sigma[r]
        for h in range(HEADS):
            cq = slice(h * HD, (h + 1) * HD)
            ck = slice(LOCAL + h * HD, LOCAL + (h + 1) * HD)
            cv = slice(2 * LOCAL + h * HD, 2 * LOCAL + (h + 1) * HD)
            d = d_mixed[r, :, cq]
            p = probs[m, h]
            dqkv[m, :, cv] = tn(p.astype(BF16), d).astype(BF16)
            d_probs = nt(d, qkv[m, :, cv])
            delta = jnp.sum(p * d_probs, axis=-1, keepdims=True)
            d_scores = (p * (d_probs - delta) * SCALE).astype(BF16)
            dqkv[m, :, cq] = nn(d_scores, qkv[m, :, ck]).astype(BF16)
            dqkv[m, :, ck] = tn(d_scores, qkv[m, :, cq]).astype(BF16)
        return carry

    lax.fori_loop(0, 8, attend, 0)


def back(sigma, wo, qkv, probs, parts):
    return pl.pallas_call(
        back_kernel,
        out_shape=jax.ShapeDtypeStruct((8, TOK, 3 * LOCAL), BF16),
        in_specs=[SMEM] + [VMEM] * 3 + [ANY] * 10,
        out_specs=VMEM,
        scratch_shapes=[
            pltpu.VMEM((8, TOK, D), BF16),
            pltpu.VMEM((8, TOK, LOCAL), BF16),
            pltpu.SemaphoreType.DMA((10,)),
        ],
        compiler_params=params(),
        cost_estimate=cost(3e9, 14e6),
        name="back",
    )(sigma, wo, qkv, probs, *parts)


def inward_kernel(dqkv, wq, wk, wv, normed, gain, *rest):
    outs, gain_part = rest[:7], rest[7]
    flat = dqkv[...].reshape(8 * TOK, 3 * LOCAL)
    total = nt(flat[:, :LOCAL], wq[0])
    total = total + nt(flat[:, LOCAL : 2 * LOCAL], wk[0])
    total = total + nt(flat[:, 2 * LOCAL :], wv[0])
    rows = normed[...].reshape(8 * TOK, TILE).astype(F32)
    gain_part[...] = jnp.sum(total * rows, axis=0, keepdims=True) / gain[...].astype(F32)
    store_pieces(outs, total.reshape(8, TOK, TILE))


def inward(dqkv, wq, wk, wv, normed, gain):
    weight = pl.BlockSpec((1, TILE, LOCAL), lambda n: (0, n, 0))
    line = pl.BlockSpec((1, TILE), lambda n: (0, n))
    return pl.pallas_call(
        inward_kernel,
        grid=(D // TILE,),
        out_shape=piece_shapes() + (jax.ShapeDtypeStruct((1, D), F32),),
        in_specs=[
            pl.BlockSpec((8, TOK, 3 * LOCAL), lambda n: (0, 0, 0)),
            weight,
            weight,
            weight,
            pl.BlockSpec((8, TOK, TILE), lambda n: (0, 0, n)),
            line,
        ],
        out_specs=piece_specs() + (line,),
        compiler_params=params(),
        cost_estimate=cost(6e9, 20e6),
        name="inward",
    )(dqkv, wq, wk, wv, normed, gain)


def out_grad_kernel(sent, *rest):
    parts, out = rest[:10], rest[10]
    grads = rest[11]
    for k, (number, row, rows) in enumerate(WHERE):
        grads[number, row : row + rows] = parts[k][...]
    out[0] = tn(
        sent[...].reshape(8 * TOK, LOCAL), grads[...].reshape(8 * TOK, TILE)
    ).astype(BF16)


def out_grad(sent, parts):
    return pl.pallas_call(
        out_grad_kernel,
        grid=(D // TILE,),
        out_shape=jax.ShapeDtypeStruct((1, LOCAL, D), BF16),
        in_specs=[pl.BlockSpec((8, TOK, LOCAL), lambda n: (0, 0, 0))]
        + [pl.BlockSpec((rows, TILE), lambda n: (0, n)) for _, _, rows in WHERE],
        out_specs=pl.BlockSpec((1, LOCAL, TILE), lambda n: (0, 0, n)),
        scratch_shapes=[pltpu.VMEM((8, TOK, TILE), BF16)],
        compiler_params=params(),
        cost_estimate=cost(2e9, 8e6),
        name="out_grad",
    )(sent, *parts)


def weight_grad_kernel(normed, dqkv, gq, gk, gv):
    rows = normed[...].reshape(8 * TOK, TILE)
    flat = dqkv[...].reshape(8 * TOK, 3 * LOCAL)
    total = tn(rows, flat).astype(BF16)
    gq[0] = total[:, :LOCAL]
    gk[0] = total[:, LOCAL : 2 * LOCAL]
    gv[0] = total[:, 2 * LOCAL :]


def weight_grad(normed, dqkv):
    out = pl.BlockSpec((1, TILE, LOCAL), lambda n: (0, n, 0))
    return pl.pallas_call(
        weight_grad_kernel,
        grid=(D // TILE,),
        out_shape=(jax.ShapeDtypeStruct((1, D, LOCAL), BF16),) * 3,
        in_specs=[
            pl.BlockSpec((8, TOK, TILE), lambda n: (0, 0, n)),
            pl.BlockSpec((8, TOK, 3 * LOCAL), lambda n: (0, 0, 0)),
        ],
        out_specs=(out,) * 3,
        compiler_params=params(),
        cost_estimate=cost(6e9, 14e6),
        name="weight_grad",
    )(normed, dqkv)


def add(a, b):
    return (a.astype(F32) + b.astype(F32)).astype(BF16)


def ring_sum(u_up, u_down, v_up, v_down, k_up, k_down):
    got_up = moved(u_up, 0, 0, 1)
    got_down = moved(u_down, 0, 0, -1)
    high_a = moved(v_up, 0, 0, 1)
    low_a = moved(v_down, 0, 0, -1)
    low_b = moved(add(k_up, got_up), 0, 0, 1)
    high_b = moved(add(k_down, got_down), 0, 0, -1)
    return low_a, low_b, high_a, high_b


def summed(own, low_a, low_b, high_a, high_b, dx):
    low = own[dx, :HALF].astype(F32) + low_a[dx].astype(F32) + low_b[dx].astype(F32)
    high = own[dx, HALF:].astype(F32) + high_a[dx].astype(F32) + high_b[dx].astype(F32)
    return low, high


def end_forward_kernel(own, low_a, low_b, high_a, high_b, same, other):
    for dx, out in enumerate((same, other)):
        low, high = summed(own, low_a, low_b, high_a, high_b, dx)
        out[:HALF] = low.astype(BF16)
        out[HALF:] = high.astype(BF16)


def end_forward(*pieces):
    return pl.pallas_call(
        end_forward_kernel,
        out_shape=(jax.ShapeDtypeStruct((TOK, D), BF16),) * 2,
        in_specs=[VMEM] * 5,
        out_specs=(VMEM, VMEM),
        compiler_params=params(),
        cost_estimate=cost(1e6, 4e6),
        name="end_forward",
    )(*pieces)


def end_back_kernel(sigma, gain, enter_same, enter_other, own, low_a, low_b, high_a, high_b, *rest):
    parts = rest[:10]
    same, other, d_out, sems = rest[10:]
    wanted = jnp.int32(0)
    for r in range(8):
        wanted = wanted + jnp.where(sigma[r] == 0, r, 0)
    load_one(parts, wanted, d_out, sems)
    gain_row = gain[...].astype(F32)
    for dx, (enter, out) in enumerate(((enter_same, same), (enter_other, other))):
        halves = summed(own, low_a, low_b, high_a, high_b, dx)
        for start, d_normed in zip((0, HALF), halves, strict=True):
            rows = slice(start, start + HALF)
            act = enter[rows].astype(F32)
            inv_rms = lax.rsqrt(jnp.mean(act * act, axis=-1, keepdims=True) + eps)
            unit = act * inv_rms
            scaled = d_normed * gain_row
            d_act = inv_rms * (scaled - unit * jnp.mean(scaled * unit, axis=-1, keepdims=True))
            if dx == 0:
                d_act = d_act + d_out[rows].astype(F32)
            out[rows] = d_act.astype(BF16)


def end_back(sigma, gain, enter_same, enter_other, pieces, parts):
    return pl.pallas_call(
        end_back_kernel,
        out_shape=(jax.ShapeDtypeStruct((TOK, D), BF16),) * 2,
        in_specs=[SMEM] + [VMEM] * 8 + [ANY] * 10,
        out_specs=(VMEM, VMEM),
        scratch_shapes=[pltpu.VMEM((TOK, D), BF16), pltpu.SemaphoreType.DMA((10,))],
        compiler_params=params(),
        cost_estimate=cost(1e6, 6e6),
        name="end_back",
    )(sigma, gain, enter_same, enter_other, *pieces, *parts)


def sum_over_peers(value):
    value = value + moved(value, 0, 1, 0)
    pairs = [
        ((s * 2 + x) * RING + z, (s * 2 + x) * RING + (z ^ 1))
        for s in range(SECTIONS)
        for x in range(2)
        for z in range(RING)
    ]
    value = value + lax.ppermute(value, ("section", "peer"), pairs)
    return value + moved(value, 0, 0, 2)


def per_device(inputs, wiring, lengths, norm_gain, w_query, w_key, w_value, w_out, cotangent):
    peer = lax.axis_index("peer")
    ids = jnp.stack([lax.axis_index("section"), peer // RING, peer % RING]).astype(jnp.int32)
    entering = gather_all(inputs[0, 0], 1)
    later = gather_all(cotangent[0, 0], -1)
    entering_parts = [part[0] for part in entering]
    later_parts = [part[0] for part in later]
    sigma, normed, qkv, probs, mixed = forward(
        ids, wiring, lengths, norm_gain, w_query, w_key, w_value, entering_parts
    )
    *cut, own, sent = outward(sigma, mixed, w_out, entering_parts)
    same, other = end_forward(own, *ring_sum(*cut))
    final_out = add(moved(same, 1, 0, 0), moved(other, 1, 1, 0))

    dqkv = back(sigma, w_out, qkv, probs, later_parts)
    *cut, own, gain_part = inward(dqkv, w_query, w_key, w_value, normed, norm_gain)
    w_out_grad = out_grad(sent, later_parts)
    w_query_grad, w_key_grad, w_value_grad = weight_grad(normed, dqkv)
    gain_grad = sum_over_peers(gain_part)
    same, other = end_back(
        sigma, norm_gain, entering_parts[0], entering_parts[1], (own, *ring_sum(*cut)), later_parts
    )
    input_grad = add(moved(same, -1, 0, 0), moved(other, -1, 1, 0))
    return (
        final_out[None, None],
        input_grad[None, None],
        gain_grad,
        w_query_grad,
        w_key_grad,
        w_value_grad,
        w_out_grad,
    )


def solution(mesh):
    return jax.shard_map(
        per_device,
        mesh=mesh,
        in_specs=(
            P("section", "peer", None, None),
            P(),
            P(),
            P("section", None),
            P("section", None, "peer"),
            P("section", None, "peer"),
            P("section", None, "peer"),
            P("section", "peer", None),
            P("section", "peer", None, None),
        ),
        out_specs=(
            P("section", "peer", None, None),
            P("section", "peer", None, None),
            P("section", None),
            P("section", None, "peer"),
            P("section", None, "peer"),
            P("section", None, "peer"),
            P("section", "peer", None),
        ),
        check_vma=False,
    )
```

```python
import functools
import math

import jax
import jax.numpy as jnp
from jax import lax
from jax.experimental import pallas as pl
from jax.experimental.pallas import tpu as pltpu
from jax.sharding import PartitionSpec as P

HD = 128
TOK = 128
HEADS = 3
LOCAL = HEADS * HD
D = 2560
SECTIONS = 16
RING = 4
SCALE = 1.0 / math.sqrt(HD)
eps = 1e-05

F32 = jnp.float32
BF16 = jnp.bfloat16
VMEM_LIMIT = 24 * 1024 * 1024


def moved(value, by_section, flip, by_ring):
    pairs = []
    for section in range(SECTIONS):
        for side in range(2):
            for place in range(RING):
                source = (section * 2 + side) * RING + place
                target = ((section + by_section) % SECTIONS * 2 + (side ^ flip)) * RING
                pairs.append((source, target + (place + by_ring) % RING))
    return lax.ppermute(value, ("section", "peer"), pairs)


def after(values, earlier):
    return lax.optimization_barrier((values, earlier))[0]


def nt(a, b):
    return lax.dot_general(a, b, (((1,), (1,)), ((), ())), preferred_element_type=F32)


def tn(a, b):
    return lax.dot_general(a, b, (((0,), (0,)), ((), ())), preferred_element_type=F32)


def nn(a, b):
    return jnp.dot(a, b, preferred_element_type=F32)


def load_one(refs, wanted, target, sem):
    for r, ref in enumerate(refs):

        @pl.when(wanted == r)
        def _(ref=ref):
            copy = pltpu.make_async_copy(ref, target, sem)
            copy.start()
            copy.wait()


def absolute(ids, r):
    dz, dx = r // 2, r % 2
    return lax.rem(ids[1] + dx, 2) * RING + lax.rem(ids[2] + dz, RING)


def forward_kernel(dz, ids, wiring, lengths, gain, wq, wk, wv, *rest):
    parts, rest = rest[:2], rest[2:]
    if dz == 0:
        sigma, normed, qkv, probs, mixed, entering, weights, sems = rest
    else:
        normed, qkv, probs, mixed, entering, weights, sems = rest[3:]
    section = ids[0]
    before = lax.rem(section + SECTIONS - 1, SECTIONS)
    w_copies = [
        pltpu.make_async_copy(w.at[0], weights.at[:, pl.ds(c * LOCAL, LOCAL)], sems.at[2 + c])
        for c, w in enumerate((wq, wk, wv))
    ]
    copies = [
        pltpu.make_async_copy(part, entering.at[dx], sems.at[dx]) for dx, part in enumerate(parts)
    ]
    for copy in copies + w_copies:
        copy.start()
    if dz == 0:
        for r in range(8):
            slot = absolute(ids, r)
            found = jnp.int32(0)
            for m in range(8):
                goes_to = wiring[1, section, wiring[0, before, absolute(ids, m)]]
                found = found + jnp.where(goes_to == slot, m, 0)
            sigma[r] = found
    for copy in copies:
        copy.wait()
    gain_row = gain[...].astype(F32)

    def norm_one(i, carry):
        at = pl.ds(pl.multiple_of(i * 32, 32), 32)
        for dx in range(2):
            act = entering[dx, at].astype(F32)
            inv_rms = lax.rsqrt(jnp.mean(act * act, axis=-1, keepdims=True) + eps)
            normed[dx, at] = (act * inv_rms * gain_row).astype(BF16)
        return carry

    lax.fori_loop(0, TOK // 32, norm_one, 0)
    for copy in w_copies:
        copy.wait()
    rows = normed[...].reshape(2 * TOK, D)
    qkv[...] = nn(rows, weights[...]).astype(BF16).reshape(2, TOK, 3 * LOCAL)
    row = lax.broadcasted_iota(jnp.int32, (TOK, TOK), 0)
    col = lax.broadcasted_iota(jnp.int32, (TOK, TOK), 1)
    for dx in range(2):
        seq_len = lengths[before, absolute(ids, 2 * dz + dx)]
        allowed = (row >= col) & (col < seq_len)
        for h in range(HEADS):
            q = qkv[dx, :, h * HD : (h + 1) * HD]
            k = qkv[dx, :, LOCAL + h * HD : LOCAL + (h + 1) * HD]
            v = qkv[dx, :, 2 * LOCAL + h * HD : 2 * LOCAL + (h + 1) * HD]
            scores = jnp.where(allowed, nt(q, k) * SCALE, -1e30)
            exp_scores = jnp.exp(scores - jnp.max(scores, axis=-1, keepdims=True))
            p = exp_scores / jnp.sum(exp_scores, axis=-1, keepdims=True)
            probs[dx, h] = p
            mixed[dx, :, h * HD : (h + 1) * HD] = nn(p.astype(BF16), v).astype(BF16)


ANY = pl.BlockSpec(memory_space=pl.ANY)
SMEM = pl.BlockSpec(memory_space=pltpu.SMEM)
VMEM = pl.BlockSpec(memory_space=pltpu.VMEM)


def params(**more):
    return pltpu.CompilerParams(vmem_limit_bytes=VMEM_LIMIT, **more)


NO_COST = pl.CostEstimate(flops=0, bytes_accessed=0, transcendentals=0)


def forward(dz, ids, wiring, lengths, gain, wq, wk, wv, parts, kept):
    shapes = [
        jax.ShapeDtypeStruct((8, TOK, 3 * LOCAL), BF16),
        jax.ShapeDtypeStruct((8, HEADS, TOK, TOK), F32),
        jax.ShapeDtypeStruct((8, TOK, LOCAL), BF16),
    ]
    specs = [
        pl.BlockSpec((2,) + shape.shape[1:], lambda i, n=len(shape.shape): (dz,) + (0,) * (n - 1))
        for shape in shapes
    ]
    shapes = [jax.ShapeDtypeStruct((2, TOK, D), BF16)] + shapes
    specs = [pl.BlockSpec((2, TOK, D), lambda i: (0, 0, 0))] + specs
    if dz == 0:
        shapes, specs = [jax.ShapeDtypeStruct((8,), jnp.int32)] + shapes, [SMEM] + specs
    return pl.pallas_call(
        functools.partial(forward_kernel, dz),
        grid=(1,),
        out_shape=shapes,
        in_specs=[SMEM] * 3 + [pl.BlockSpec((1, D), lambda i: (0, 0))] + [ANY] * (5 + len(kept)),
        out_specs=specs,
        input_output_aliases={9 + i: 1 + i for i in range(len(kept))},
        scratch_shapes=[
            pltpu.VMEM((2, TOK, D), BF16),
            pltpu.VMEM((D, 3 * LOCAL), BF16),
            pltpu.SemaphoreType.DMA((5,)),
        ],
        compiler_params=params(),
        cost_estimate=NO_COST,
        name="forward",
    )(ids, wiring, lengths, gain, wq, wk, wv, *parts[2 * dz : 2 * dz + 2], *kept)


TILE = 512


def store_pieces(outs, total):
    for r, out in enumerate(outs):
        out[...] = total[r].astype(BF16)


def piece_shapes():
    return (jax.ShapeDtypeStruct((TOK, D), BF16),) * 8


def piece_specs():
    return (pl.BlockSpec((TOK, TILE), lambda n: (0, n)),) * 8


def outward_kernel(sigma, mixed, wo, *rest):
    parts, outs, sent = rest[:8], rest[8:16], rest[16]
    entering, sem = rest[17:]
    tile = pl.program_id(0)

    @pl.when(tile == 0)
    def _():
        for r in range(8):
            sent[r] = mixed[sigma[r]]
        load_one(parts, sigma[0], entering, sem)

    total = nn(sent[...].reshape(8 * TOK, LOCAL), wo[0]).reshape(8, TOK, TILE)
    store_pieces(outs[1:], total[1:])
    residual = entering[:, pl.ds(pl.multiple_of(tile * TILE, TILE), TILE)].astype(F32)
    outs[0][...] = (total[0] + residual).astype(BF16)


def outward(sigma, mixed, wo, parts):
    whole = pl.BlockSpec((8, TOK, LOCAL), lambda n: (0, 0, 0))
    return pl.pallas_call(
        outward_kernel,
        grid=(D // TILE,),
        out_shape=piece_shapes() + (jax.ShapeDtypeStruct((8, TOK, LOCAL), BF16),),
        in_specs=[SMEM, whole, pl.BlockSpec((1, LOCAL, TILE), lambda n: (0, 0, n))] + [ANY] * 8,
        out_specs=piece_specs() + (whole,),
        scratch_shapes=[pltpu.VMEM((TOK, D), BF16), pltpu.SemaphoreType.DMA(())],
        compiler_params=params(),
        cost_estimate=NO_COST,
        name="outward",
    )(sigma, mixed, wo, *parts)


def back_kernel(dz, sigma, wo, qkv, probs, *rest):
    parts = rest[:2]
    dqkv, grads, d_mixed, heads, soft, sems = rest[-6:]
    copies = [
        pltpu.make_async_copy(part, grads.at[dx], sems.at[dx]) for dx, part in enumerate(parts)
    ]
    for dx in range(2):
        m = sigma[2 * dz + dx]
        copies.append(pltpu.make_async_copy(qkv.at[m], heads.at[dx], sems.at[2 + dx]))
        copies.append(pltpu.make_async_copy(probs.at[m], soft.at[dx], sems.at[4 + dx]))
    for copy in copies:
        copy.start()
    for copy in copies:
        copy.wait()
    rows = grads[...].reshape(2 * TOK, D)
    d_mixed[...] = nt(rows, wo[0]).astype(BF16).reshape(2, TOK, LOCAL)
    for dx in range(2):
        for h in range(HEADS):
            cq = slice(h * HD, (h + 1) * HD)
            ck = slice(LOCAL + h * HD, LOCAL + (h + 1) * HD)
            cv = slice(2 * LOCAL + h * HD, 2 * LOCAL + (h + 1) * HD)
            d = d_mixed[dx, :, cq]
            p = soft[dx, h]
            dqkv[dx, :, cv] = tn(p.astype(BF16), d).astype(BF16)
            d_probs = nt(d, heads[dx, :, cv])
            delta = jnp.sum(p * d_probs, axis=-1, keepdims=True)
            d_scores = (p * (d_probs - delta) * SCALE).astype(BF16)
            dqkv[dx, :, cq] = nn(d_scores, heads[dx, :, ck]).astype(BF16)
            dqkv[dx, :, ck] = tn(d_scores, heads[dx, :, cq]).astype(BF16)


def back(dz, sigma, wo, qkv, probs, parts, kept):
    return pl.pallas_call(
        functools.partial(back_kernel, dz),
        grid=(1,),
        out_shape=jax.ShapeDtypeStruct((8, TOK, 3 * LOCAL), BF16),
        in_specs=[SMEM, pl.BlockSpec((1, LOCAL, D), lambda i: (0, 0, 0))] + [ANY] * (4 + len(kept)),
        out_specs=pl.BlockSpec((2, TOK, 3 * LOCAL), lambda i: (dz, 0, 0)),
        input_output_aliases={6 + i: i for i in range(len(kept))},
        scratch_shapes=[
            pltpu.VMEM((2, TOK, D), BF16),
            pltpu.VMEM((2, TOK, LOCAL), BF16),
            pltpu.VMEM((2, TOK, 3 * LOCAL), BF16),
            pltpu.VMEM((2, HEADS, TOK, TOK), F32),
            pltpu.SemaphoreType.DMA((6,)),
        ],
        compiler_params=params(),
        cost_estimate=NO_COST,
        name="back",
    )(sigma, wo, qkv, probs, *parts[2 * dz : 2 * dz + 2], *kept)


def inward_kernel(numbers, sigma, dqkv, wq, wk, wv, *rest):
    outs, (flat, weights) = rest[: len(numbers)], rest[-2:]
    count = len(numbers)

    @pl.when(pl.program_id(0) == 0)
    def _():
        for r in range(8):
            if count == 8:
                flat[sigma[r]] = dqkv[r]
                continue
            for i, number in enumerate(numbers):

                @pl.when(sigma[r] == number)
                def _(r=r, i=i):
                    flat[i] = dqkv[r]

        if len(rest) > count + 2:
            for r in range(8):
                rest[count][sigma[r]] = dqkv[r]

    for c, w in enumerate((wq, wk, wv)):
        weights[:, c * LOCAL : (c + 1) * LOCAL] = w[0]
    total = nt(flat[...].reshape(count * TOK, 3 * LOCAL), weights[...])
    store_pieces(outs, total.reshape(count, TOK, TILE))


def inward(numbers, in_order, sigma, dqkv, wq, wk, wv):
    weight = pl.BlockSpec((1, TILE, LOCAL), lambda n: (0, n, 0))
    whole = pl.BlockSpec((8, TOK, 3 * LOCAL), lambda n: (0, 0, 0))
    count = len(numbers)
    return pl.pallas_call(
        functools.partial(inward_kernel, numbers),
        grid=(D // TILE,),
        out_shape=piece_shapes()[:count]
        + (jax.ShapeDtypeStruct((8, TOK, 3 * LOCAL), BF16),) * in_order,
        in_specs=[SMEM, whole, weight, weight, weight],
        out_specs=piece_specs()[:count] + (whole,) * in_order,
        scratch_shapes=[
            pltpu.VMEM((count, TOK, 3 * LOCAL), BF16),
            pltpu.VMEM((TILE, 3 * LOCAL), BF16),
        ],
        compiler_params=params(),
        cost_estimate=NO_COST,
        name="inward",
    )(sigma, dqkv, wq, wk, wv)


def out_grad_kernel(sent, *rest):
    parts, out, grads = rest[:8], rest[8], rest[9]
    for r, part in enumerate(parts):
        grads[r] = part[...]
    out[0] = tn(
        sent[...].reshape(8 * TOK, LOCAL), grads[...].reshape(8 * TOK, TILE)
    ).astype(BF16)


def out_grad(sent, parts):
    return pl.pallas_call(
        out_grad_kernel,
        grid=(D // TILE,),
        out_shape=jax.ShapeDtypeStruct((1, LOCAL, D), BF16),
        in_specs=[pl.BlockSpec((8, TOK, LOCAL), lambda n: (0, 0, 0))] + list(piece_specs()),
        out_specs=pl.BlockSpec((1, LOCAL, TILE), lambda n: (0, 0, n)),
        scratch_shapes=[pltpu.VMEM((8, TOK, TILE), BF16)],
        compiler_params=params(),
        cost_estimate=NO_COST,
        name="out_grad",
    )(sent, *parts)


def weight_grad_kernel(n0, n1, n2, n3, dqkv, wq, wk, wv, gain, gq, gk, gv, gain_part, rows):
    for dz, n in enumerate((n0, n1, n2, n3)):
        rows[2 * dz : 2 * dz + 2] = n[...]
    flat = dqkv[...].reshape(8 * TOK, 3 * LOCAL)
    total = tn(rows[...].reshape(8 * TOK, TILE), flat)
    along = jnp.zeros((TILE, 1), F32)
    for c, (w, g) in enumerate(((wq, gq), (wk, gk), (wv, gv))):
        part = total[:, c * LOCAL : (c + 1) * LOCAL]
        along = along + jnp.sum(part * w[0].astype(F32), axis=1, keepdims=True)
        g[0] = part.astype(BF16)
    gain_part[...] = along.T / gain[...].astype(F32)


def weight_grad(normed, dqkv, wq, wk, wv, gain):
    tile = pl.BlockSpec((1, TILE, LOCAL), lambda n: (0, n, 0))
    line = pl.BlockSpec((1, TILE), lambda n: (0, n))
    return pl.pallas_call(
        weight_grad_kernel,
        grid=(D // TILE,),
        out_shape=(jax.ShapeDtypeStruct((1, D, LOCAL), BF16),) * 3
        + (jax.ShapeDtypeStruct((1, D), F32),),
        in_specs=[pl.BlockSpec((2, TOK, TILE), lambda n: (0, 0, n))] * 4
        + [pl.BlockSpec((8, TOK, 3 * LOCAL), lambda n: (0, 0, 0))]
        + [tile] * 3
        + [line],
        out_specs=(tile,) * 3 + (line,),
        scratch_shapes=[pltpu.VMEM((8, TOK, TILE), BF16)],
        compiler_params=params(),
        cost_estimate=NO_COST,
        name="weight_grad",
    )(*normed, dqkv, wq, wk, wv, gain)


def sum_kernel(*refs):
    total = refs[0][...].astype(F32)
    for ref in refs[1:-1]:
        total = total + ref[...].astype(F32)
    refs[-1][...] = total.astype(BF16)


def summed(*values):
    return pl.pallas_call(
        sum_kernel,
        grid=(1,),
        out_shape=jax.ShapeDtypeStruct((TOK, D), BF16),
        in_specs=[pl.BlockSpec((TOK, D), lambda n, b=block: (b, 0)) for _, block in values],
        out_specs=pl.BlockSpec((TOK, D), lambda n: (0, 0)),
        compiler_params=params(),
        cost_estimate=NO_COST,
        name="summed",
    )(*[value for value, _ in values])


def add(a, b):
    return summed((a, 0), (b, 0))


def add_three(a, b, c):
    return summed((a, 0), (b, 0), (c, 0))


def pick_kernel(sigma, *refs):
    parts, out, sem = refs[:8], refs[8], refs[9]
    wanted = jnp.int32(0)
    for r in range(8):
        wanted = wanted + jnp.where(sigma[r] == 0, r, 0)
    load_one(parts, wanted, out, sem)


def pick(sigma, parts):
    return pl.pallas_call(
        pick_kernel,
        out_shape=jax.ShapeDtypeStruct((TOK, D), BF16),
        in_specs=[SMEM] + [ANY] * 8,
        out_specs=ANY,
        scratch_shapes=[pltpu.SemaphoreType.DMA(())],
        compiler_params=params(),
        cost_estimate=NO_COST,
        name="pick",
    )(sigma, *parts)


def end_back_kernel(gain, enter, a, b, c, *rest):
    out = rest[-1]
    gain_row = gain[...].astype(F32)
    for i in range(4):
        rows = slice(i * 32, (i + 1) * 32)
        d_normed = a[rows].astype(F32) + b[rows].astype(F32) + c[rows].astype(F32)
        act = enter[rows].astype(F32)
        inv_rms = lax.rsqrt(jnp.mean(act * act, axis=-1, keepdims=True) + eps)
        unit = act * inv_rms
        scaled = d_normed * gain_row
        d_act = inv_rms * (scaled - unit * jnp.mean(scaled * unit, axis=-1, keepdims=True))
        if len(rest) == 2:
            d_act = d_act + rest[0][rows].astype(F32)
        out[rows] = d_act.astype(BF16)


def end_back(gain, enter, pieces, *residual):
    return pl.pallas_call(
        end_back_kernel,
        out_shape=jax.ShapeDtypeStruct((TOK, D), BF16),
        in_specs=[VMEM] * (5 + len(residual)),
        out_specs=VMEM,
        compiler_params=params(),
        cost_estimate=NO_COST,
        name="end_back",
    )(gain, enter, *pieces, *residual)


def paired(value):
    pairs = [(i, i ^ 1) for i in range(SECTIONS * 2 * RING)]
    return lax.ppermute(value, ("section", "peer"), pairs)


def per_device(inputs, wiring, lengths, norm_gain, w_query, w_key, w_value, w_out, cotangent):
    peer = lax.axis_index("peer")
    ids = jnp.stack([lax.axis_index("section"), peer // RING, peer % RING]).astype(jnp.int32)
    here, there = inputs[0, 0], cotangent[0, 0]
    e, g = [None] * 8, [None] * 8
    normed, kept, sigma = [None] * 4, (), None

    def run_forward(dz, earlier):
        nonlocal kept, sigma
        *first, normed[dz], qkv, probs, mixed = forward(
            dz, after(ids, earlier), wiring, lengths, norm_gain, w_query, w_key, w_value, e, kept
        )
        kept = (qkv, probs, mixed)
        if dz == 0:
            sigma = first[0]

    def both(value_up, value_down, earlier):
        value_up, value_down = after((value_up, value_down), earlier)
        return moved(value_up, 0, 0, 1), moved(value_down, 0, 0, -1)

    e[0], e[1] = moved(here, 1, 0, 0), moved(here, 1, 1, 0)
    e[6], e[2] = both(e[0], e[0], ())
    g[0], g[1] = moved(after(there, e[0]), -1, 0, 0), moved(after(there, e[0]), -1, 1, 0)
    e[7], e[3] = both(e[1], e[1], ())
    run_forward(0, ())
    g[6], g[2] = both(g[0], g[0], (e[6], e[2], normed[0]))
    e[4], e[5] = both(e[6], e[3], (e[7],))
    run_forward(1, (e[7],))
    g[7], g[3] = both(g[1], g[1], (g[6], g[2], normed[1]))
    run_forward(3, (g[6], g[2]))
    run_forward(2, ())
    qkv, probs, mixed = kept
    g[4] = moved(after(g[2], (e[5], normed[3])), 0, 0, -1)
    *piece, sent = outward(sigma, mixed, w_out, e)
    dqkv = ()

    def run_back(dz, earlier):
        nonlocal dqkv
        dqkv = (back(dz, after(sigma, earlier), w_out, qkv, probs, g, dqkv),)

    up, down = both(piece[4], piece[5], (g[7], g[3]))
    run_back(0, (sent, g[7], g[3]))
    got_1, got_0 = both(piece[3], piece[6], dqkv)
    g[5] = moved(after(g[4], dqkv), 0, 1, 0)
    run_back(1, ())
    run_back(3, ())
    up, down = after((up, down), dqkv)
    last_0, last_1 = both(add(piece[2], up), add(piece[7], down), ())
    run_back(2, ())
    first_0, first_1 = (piece[0], got_0, last_0), (piece[1], got_1, last_1)
    dqkv, weights = dqkv[0], (w_query, w_key, w_value)
    piece = [None] * 8
    now = after(sigma, (got_0, got_1))
    piece[4], piece[5] = inward((4, 5), False, now, dqkv, *weights)
    up, down = moved(piece[4], 0, 0, 1), moved(piece[5], 0, 0, -1)
    rest = (3, 6, 7, 2, 0, 1)
    *pieces, dqkv = inward(rest, True, after(now, piece[4]), dqkv, *weights)
    for r, value in zip(rest, pieces, strict=True):
        piece[r] = value
    got_1, got_0 = moved(piece[3], 0, 0, 1), moved(piece[6], 0, 0, -1)
    first_0, first_1 = after((first_0, first_1), dqkv)
    w_query_grad, w_key_grad, w_value_grad, gain_part = weight_grad(
        normed, after(dqkv, (first_0, first_1)), *weights, norm_gain
    )
    other = moved(add_three(*first_1), 1, 1, 0)
    same = moved(add_three(*first_0), 1, 0, 0)
    up, down = after(up, w_query_grad), after(down, w_query_grad)
    last_1 = moved(add(piece[7], down), 0, 0, -1)
    last_0 = moved(add(piece[2], up), 0, 0, 1)
    w_out_grad = out_grad(after(sent, (got_1, got_0, same, other)), g)
    gain_part = gain_part + moved(after(gain_part, other), 0, 1, 0)
    gain_part = after(gain_part, w_out_grad)
    gain_part = gain_part + paired(gain_part)
    d_out = pick(after(sigma, w_out_grad), g)
    to_other = end_back(norm_gain, e[1], (piece[1], got_1, after(last_1, gain_part)))
    to_other = moved(to_other, -1, 1, 0)
    to_same = end_back(norm_gain, e[0], (piece[0], got_0, last_0), d_out)
    final_out = add(same, other)
    gain_grad = gain_part + moved(gain_part, 0, 0, 2)
    input_grad = add(moved(to_same, -1, 0, 0), after(to_other, (gain_grad, final_out)))
    return (
        final_out[None, None],
        input_grad[None, None],
        gain_grad,
        w_query_grad,
        w_key_grad,
        w_value_grad,
        w_out_grad,
    )


def solution(mesh):
    return jax.shard_map(
        per_device,
        mesh=mesh,
        in_specs=(
            P("section", "peer", None, None),
            P(),
            P(),
            P("section", None),
            P("section", None, "peer"),
            P("section", None, "peer"),
            P("section", None, "peer"),
            P("section", "peer", None),
            P("section", "peer", None, None),
        ),
        out_specs=(
            P("section", "peer", None, None),
            P("section", "peer", None, None),
            P("section", None),
            P("section", None, "peer"),
            P("section", None, "peer"),
            P("section", None, "peer"),
            P("section", "peer", None),
        ),
        check_vma=False,
    )
```

```python
import functools
import math

import jax
import jax.numpy as jnp
from jax import lax
from jax.experimental import pallas as pl
from jax.experimental.pallas import tpu as pltpu
from jax.sharding import PartitionSpec as P

HD = 128
TOK = 128
HEADS = 3
LOCAL = HEADS * HD
D = 2560
SECTIONS = 16
RING = 4
SCALE = 1.0 / math.sqrt(HD)
eps = 1e-05

F32 = jnp.float32
BF16 = jnp.bfloat16
VMEM_LIMIT = 24 * 1024 * 1024


def moved(value, by_section, flip, by_ring):
    pairs = []
    for section in range(SECTIONS):
        for side in range(2):
            for place in range(RING):
                source = (section * 2 + side) * RING + place
                target = ((section + by_section) % SECTIONS * 2 + (side ^ flip)) * RING
                pairs.append((source, target + (place + by_ring) % RING))
    return lax.ppermute(value, ("section", "peer"), pairs)


def after(values, earlier):
    return lax.optimization_barrier((values, earlier))[0]


def nt(a, b):
    return lax.dot_general(a, b, (((1,), (1,)), ((), ())), preferred_element_type=F32)


def tn(a, b):
    return lax.dot_general(a, b, (((0,), (0,)), ((), ())), preferred_element_type=F32)


def nn(a, b):
    return jnp.dot(a, b, preferred_element_type=F32)


def load_one(refs, wanted, target, sem):
    for r, ref in enumerate(refs):

        @pl.when(wanted == r)
        def _(ref=ref):
            copy = pltpu.make_async_copy(ref, target, sem)
            copy.start()
            copy.wait()


def absolute(ids, r):
    dz, dx = r // 2, r % 2
    return lax.rem(ids[1] + dx, 2) * RING + lax.rem(ids[2] + dz, RING)


def forward_kernel(dz, ids, wiring, lengths, gain, wq, wk, wv, *rest):
    parts, rest = rest[:2], rest[2:]
    if dz == 0:
        sigma, normed, qkv, probs, mixed, entering, weights, sems = rest
    else:
        normed, qkv, probs, mixed, entering, weights, sems = rest[3:]
    section = ids[0]
    before = lax.rem(section + SECTIONS - 1, SECTIONS)
    w_copies = [
        pltpu.make_async_copy(w.at[0], weights.at[:, pl.ds(c * LOCAL, LOCAL)], sems.at[2 + c])
        for c, w in enumerate((wq, wk, wv))
    ]
    copies = [
        pltpu.make_async_copy(part, entering.at[dx], sems.at[dx]) for dx, part in enumerate(parts)
    ]
    for copy in copies + w_copies:
        copy.start()
    if dz == 0:
        for r in range(8):
            slot = absolute(ids, r)
            found = jnp.int32(0)
            for m in range(8):
                goes_to = wiring[1, section, wiring[0, before, absolute(ids, m)]]
                found = found + jnp.where(goes_to == slot, m, 0)
            sigma[r] = found
    for copy in copies:
        copy.wait()
    gain_row = gain[...].astype(F32)

    def norm_one(i, carry):
        at = pl.ds(pl.multiple_of(i * 32, 32), 32)
        for dx in range(2):
            act = entering[dx, at].astype(F32)
            inv_rms = lax.rsqrt(jnp.mean(act * act, axis=-1, keepdims=True) + eps)
            normed[dx, at] = (act * inv_rms * gain_row).astype(BF16)
        return carry

    lax.fori_loop(0, TOK // 32, norm_one, 0)
    for copy in w_copies:
        copy.wait()
    rows = normed[...].reshape(2 * TOK, D)
    qkv[...] = nn(rows, weights[...]).astype(BF16).reshape(2, TOK, 3 * LOCAL)
    row = lax.broadcasted_iota(jnp.int32, (TOK, TOK), 0)
    col = lax.broadcasted_iota(jnp.int32, (TOK, TOK), 1)
    for dx in range(2):
        seq_len = lengths[before, absolute(ids, 2 * dz + dx)]
        allowed = (row >= col) & (col < seq_len)
        for h in range(HEADS):
            q = qkv[dx, :, h * HD : (h + 1) * HD]
            k = qkv[dx, :, LOCAL + h * HD : LOCAL + (h + 1) * HD]
            v = qkv[dx, :, 2 * LOCAL + h * HD : 2 * LOCAL + (h + 1) * HD]
            scores = jnp.where(allowed, nt(q, k) * SCALE, -1e30)
            exp_scores = jnp.exp(scores - jnp.max(scores, axis=-1, keepdims=True))
            p = exp_scores / jnp.sum(exp_scores, axis=-1, keepdims=True)
            probs[dx, h] = p
            mixed[dx, :, h * HD : (h + 1) * HD] = nn(p.astype(BF16), v).astype(BF16)


ANY = pl.BlockSpec(memory_space=pl.ANY)
SMEM = pl.BlockSpec(memory_space=pltpu.SMEM)
VMEM = pl.BlockSpec(memory_space=pltpu.VMEM)


def params(**more):
    return pltpu.CompilerParams(vmem_limit_bytes=VMEM_LIMIT, **more)


NO_COST = pl.CostEstimate(flops=0, bytes_accessed=0, transcendentals=0)


def forward(dz, ids, wiring, lengths, gain, wq, wk, wv, parts, kept):
    shapes = [
        jax.ShapeDtypeStruct((8, TOK, 3 * LOCAL), BF16),
        jax.ShapeDtypeStruct((8, HEADS, TOK, TOK), F32),
        jax.ShapeDtypeStruct((8, TOK, LOCAL), BF16),
    ]
    specs = [
        pl.BlockSpec((2,) + shape.shape[1:], lambda i, n=len(shape.shape): (dz,) + (0,) * (n - 1))
        for shape in shapes
    ]
    shapes = [jax.ShapeDtypeStruct((2, TOK, D), BF16)] + shapes
    specs = [pl.BlockSpec((2, TOK, D), lambda i: (0, 0, 0))] + specs
    if dz == 0:
        shapes, specs = [jax.ShapeDtypeStruct((8,), jnp.int32)] + shapes, [SMEM] + specs
    return pl.pallas_call(
        functools.partial(forward_kernel, dz),
        grid=(1,),
        out_shape=shapes,
        in_specs=[SMEM] * 3 + [pl.BlockSpec((1, D), lambda i: (0, 0))] + [ANY] * (5 + len(kept)),
        out_specs=specs,
        input_output_aliases={9 + i: 1 + i for i in range(len(kept))},
        scratch_shapes=[
            pltpu.VMEM((2, TOK, D), BF16),
            pltpu.VMEM((D, 3 * LOCAL), BF16),
            pltpu.SemaphoreType.DMA((5,)),
        ],
        compiler_params=params(),
        cost_estimate=NO_COST,
        name="forward",
    )(ids, wiring, lengths, gain, wq, wk, wv, *parts[2 * dz : 2 * dz + 2], *kept)


TILE = 512


def store_pieces(outs, total):
    for r, out in enumerate(outs):
        out[...] = total[r].astype(BF16)


def piece_shapes():
    return (jax.ShapeDtypeStruct((TOK, D), BF16),) * 8


def piece_specs():
    return (pl.BlockSpec((TOK, TILE), lambda n: (0, n)),) * 8


def outward_kernel(sigma, mixed, wo, *rest):
    parts, outs, sent = rest[:8], rest[8:16], rest[16]
    entering, sem = rest[17:]
    tile = pl.program_id(0)

    @pl.when(tile == 0)
    def _():
        for r in range(8):
            sent[r] = mixed[sigma[r]]
        load_one(parts, sigma[0], entering, sem)

    total = nn(sent[...].reshape(8 * TOK, LOCAL), wo[0]).reshape(8, TOK, TILE)
    store_pieces(outs[1:], total[1:])
    residual = entering[:, pl.ds(pl.multiple_of(tile * TILE, TILE), TILE)].astype(F32)
    outs[0][...] = (total[0] + residual).astype(BF16)


def outward(sigma, mixed, wo, parts):
    whole = pl.BlockSpec((8, TOK, LOCAL), lambda n: (0, 0, 0))
    return pl.pallas_call(
        outward_kernel,
        grid=(D // TILE,),
        out_shape=piece_shapes() + (jax.ShapeDtypeStruct((8, TOK, LOCAL), BF16),),
        in_specs=[SMEM, whole, pl.BlockSpec((1, LOCAL, TILE), lambda n: (0, 0, n))] + [ANY] * 8,
        out_specs=piece_specs() + (whole,),
        scratch_shapes=[pltpu.VMEM((TOK, D), BF16), pltpu.SemaphoreType.DMA(())],
        compiler_params=params(),
        cost_estimate=NO_COST,
        name="outward",
    )(sigma, mixed, wo, *parts)


def back_kernel(dz, sigma, wo, qkv, probs, *rest):
    parts = rest[:2]
    dqkv, grads, d_mixed, heads, soft, sems = rest[-6:]
    copies = [
        pltpu.make_async_copy(part, grads.at[dx], sems.at[dx]) for dx, part in enumerate(parts)
    ]
    for dx in range(2):
        m = sigma[2 * dz + dx]
        copies.append(pltpu.make_async_copy(qkv.at[m], heads.at[dx], sems.at[2 + dx]))
        copies.append(pltpu.make_async_copy(probs.at[m], soft.at[dx], sems.at[4 + dx]))
    for copy in copies:
        copy.start()
    for copy in copies:
        copy.wait()
    rows = grads[...].reshape(2 * TOK, D)
    d_mixed[...] = nt(rows, wo[0]).astype(BF16).reshape(2, TOK, LOCAL)
    for dx in range(2):
        for h in range(HEADS):
            cq = slice(h * HD, (h + 1) * HD)
            ck = slice(LOCAL + h * HD, LOCAL + (h + 1) * HD)
            cv = slice(2 * LOCAL + h * HD, 2 * LOCAL + (h + 1) * HD)
            d = d_mixed[dx, :, cq]
            p = soft[dx, h]
            dqkv[dx, :, cv] = tn(p.astype(BF16), d).astype(BF16)
            d_probs = nt(d, heads[dx, :, cv])
            delta = jnp.sum(p * d_probs, axis=-1, keepdims=True)
            d_scores = (p * (d_probs - delta) * SCALE).astype(BF16)
            dqkv[dx, :, cq] = nn(d_scores, heads[dx, :, ck]).astype(BF16)
            dqkv[dx, :, ck] = tn(d_scores, heads[dx, :, cq]).astype(BF16)


def back(dz, sigma, wo, qkv, probs, parts, kept):
    return pl.pallas_call(
        functools.partial(back_kernel, dz),
        grid=(1,),
        out_shape=jax.ShapeDtypeStruct((8, TOK, 3 * LOCAL), BF16),
        in_specs=[SMEM, pl.BlockSpec((1, LOCAL, D), lambda i: (0, 0, 0))] + [ANY] * (4 + len(kept)),
        out_specs=pl.BlockSpec((2, TOK, 3 * LOCAL), lambda i: (dz, 0, 0)),
        input_output_aliases={6 + i: i for i in range(len(kept))},
        scratch_shapes=[
            pltpu.VMEM((2, TOK, D), BF16),
            pltpu.VMEM((2, TOK, LOCAL), BF16),
            pltpu.VMEM((2, TOK, 3 * LOCAL), BF16),
            pltpu.VMEM((2, HEADS, TOK, TOK), F32),
            pltpu.SemaphoreType.DMA((6,)),
        ],
        compiler_params=params(),
        cost_estimate=NO_COST,
        name="back",
    )(sigma, wo, qkv, probs, *parts[2 * dz : 2 * dz + 2], *kept)


def inward_kernel(numbers, sigma, dqkv, wq, wk, wv, *rest):
    outs, (flat, weights) = rest[: len(numbers)], rest[-2:]
    count = len(numbers)

    @pl.when(pl.program_id(0) == 0)
    def _():
        for r in range(8):
            if count == 8:
                flat[sigma[r]] = dqkv[r]
                continue
            for i, number in enumerate(numbers):

                @pl.when(sigma[r] == number)
                def _(r=r, i=i):
                    flat[i] = dqkv[r]

        if len(rest) > count + 2:
            for r in range(8):
                rest[count][sigma[r]] = dqkv[r]

    for c, w in enumerate((wq, wk, wv)):
        weights[:, c * LOCAL : (c + 1) * LOCAL] = w[0]
    total = nt(flat[...].reshape(count * TOK, 3 * LOCAL), weights[...])
    store_pieces(outs, total.reshape(count, TOK, TILE))


def inward(numbers, in_order, sigma, dqkv, wq, wk, wv):
    weight = pl.BlockSpec((1, TILE, LOCAL), lambda n: (0, n, 0))
    whole = pl.BlockSpec((8, TOK, 3 * LOCAL), lambda n: (0, 0, 0))
    count = len(numbers)
    return pl.pallas_call(
        functools.partial(inward_kernel, numbers),
        grid=(D // TILE,),
        out_shape=piece_shapes()[:count]
        + (jax.ShapeDtypeStruct((8, TOK, 3 * LOCAL), BF16),) * in_order,
        in_specs=[SMEM, whole, weight, weight, weight],
        out_specs=piece_specs()[:count] + (whole,) * in_order,
        scratch_shapes=[
            pltpu.VMEM((count, TOK, 3 * LOCAL), BF16),
            pltpu.VMEM((TILE, 3 * LOCAL), BF16),
        ],
        compiler_params=params(),
        cost_estimate=NO_COST,
        name="inward",
    )(sigma, dqkv, wq, wk, wv)


def out_grad_kernel(sent, *rest):
    parts, out, grads = rest[:8], rest[8], rest[9]
    for r, part in enumerate(parts):
        grads[r] = part[...]
    out[0] = tn(
        sent[...].reshape(8 * TOK, LOCAL), grads[...].reshape(8 * TOK, TILE)
    ).astype(BF16)


def out_grad(sent, parts):
    return pl.pallas_call(
        out_grad_kernel,
        grid=(D // TILE,),
        out_shape=jax.ShapeDtypeStruct((1, LOCAL, D), BF16),
        in_specs=[pl.BlockSpec((8, TOK, LOCAL), lambda n: (0, 0, 0))] + list(piece_specs()),
        out_specs=pl.BlockSpec((1, LOCAL, TILE), lambda n: (0, 0, n)),
        scratch_shapes=[pltpu.VMEM((8, TOK, TILE), BF16)],
        compiler_params=params(),
        cost_estimate=NO_COST,
        name="out_grad",
    )(sent, *parts)


def weight_grad_kernel(n0, n1, n2, n3, dqkv, wq, wk, wv, gain, gq, gk, gv, gain_part, rows):
    for dz, n in enumerate((n0, n1, n2, n3)):
        rows[2 * dz : 2 * dz + 2] = n[...]
    flat = dqkv[...].reshape(8 * TOK, 3 * LOCAL)
    total = tn(rows[...].reshape(8 * TOK, TILE), flat)
    along = jnp.zeros((TILE, 1), F32)
    for c, (w, g) in enumerate(((wq, gq), (wk, gk), (wv, gv))):
        part = total[:, c * LOCAL : (c + 1) * LOCAL]
        along = along + jnp.sum(part * w[0].astype(F32), axis=1, keepdims=True)
        g[0] = part.astype(BF16)
    gain_part[...] = along.T / gain[...].astype(F32)


def weight_grad(normed, dqkv, wq, wk, wv, gain):
    tile = pl.BlockSpec((1, TILE, LOCAL), lambda n: (0, n, 0))
    line = pl.BlockSpec((1, TILE), lambda n: (0, n))
    return pl.pallas_call(
        weight_grad_kernel,
        grid=(D // TILE,),
        out_shape=(jax.ShapeDtypeStruct((1, D, LOCAL), BF16),) * 3
        + (jax.ShapeDtypeStruct((1, D), F32),),
        in_specs=[pl.BlockSpec((2, TOK, TILE), lambda n: (0, 0, n))] * 4
        + [pl.BlockSpec((8, TOK, 3 * LOCAL), lambda n: (0, 0, 0))]
        + [tile] * 3
        + [line],
        out_specs=(tile,) * 3 + (line,),
        scratch_shapes=[pltpu.VMEM((8, TOK, TILE), BF16)],
        compiler_params=params(),
        cost_estimate=NO_COST,
        name="weight_grad",
    )(*normed, dqkv, wq, wk, wv, gain)


def sum_kernel(*refs):
    total = refs[0][...].astype(F32)
    for ref in refs[1:-1]:
        total = total + ref[...].astype(F32)
    refs[-1][...] = total.astype(BF16)


def summed(*values):
    return pl.pallas_call(
        sum_kernel,
        grid=(1,),
        out_shape=jax.ShapeDtypeStruct((TOK, D), BF16),
        in_specs=[pl.BlockSpec((TOK, D), lambda n, b=block: (b, 0)) for _, block in values],
        out_specs=pl.BlockSpec((TOK, D), lambda n: (0, 0)),
        compiler_params=params(),
        cost_estimate=NO_COST,
        name="summed",
    )(*[value for value, _ in values])


def add(a, b):
    return summed((a, 0), (b, 0))


def add_three(a, b, c):
    return summed((a, 0), (b, 0), (c, 0))


def pick_kernel(sigma, *refs):
    parts, out, sem = refs[:8], refs[8], refs[9]
    wanted = jnp.int32(0)
    for r in range(8):
        wanted = wanted + jnp.where(sigma[r] == 0, r, 0)
    load_one(parts, wanted, out, sem)


def pick(sigma, parts):
    return pl.pallas_call(
        pick_kernel,
        out_shape=jax.ShapeDtypeStruct((TOK, D), BF16),
        in_specs=[SMEM] + [ANY] * 8,
        out_specs=ANY,
        scratch_shapes=[pltpu.SemaphoreType.DMA(())],
        compiler_params=params(),
        cost_estimate=NO_COST,
        name="pick",
    )(sigma, *parts)


def end_back_kernel(gain, enter, a, b, c, *rest):
    out = rest[-1]
    gain_row = gain[...].astype(F32)
    for i in range(4):
        rows = slice(i * 32, (i + 1) * 32)
        d_normed = a[rows].astype(F32) + b[rows].astype(F32) + c[rows].astype(F32)
        act = enter[rows].astype(F32)
        inv_rms = lax.rsqrt(jnp.mean(act * act, axis=-1, keepdims=True) + eps)
        unit = act * inv_rms
        scaled = d_normed * gain_row
        d_act = inv_rms * (scaled - unit * jnp.mean(scaled * unit, axis=-1, keepdims=True))
        if len(rest) == 2:
            d_act = d_act + rest[0][rows].astype(F32)
        out[rows] = d_act.astype(BF16)


def end_back(gain, enter, pieces, *residual):
    return pl.pallas_call(
        end_back_kernel,
        out_shape=jax.ShapeDtypeStruct((TOK, D), BF16),
        in_specs=[VMEM] * (5 + len(residual)),
        out_specs=VMEM,
        compiler_params=params(),
        cost_estimate=NO_COST,
        name="end_back",
    )(gain, enter, *pieces, *residual)


def paired(value):
    pairs = [(i, i ^ 1) for i in range(SECTIONS * 2 * RING)]
    return lax.ppermute(value, ("section", "peer"), pairs)


def per_device(inputs, wiring, lengths, norm_gain, w_query, w_key, w_value, w_out, cotangent):
    peer = lax.axis_index("peer")
    ids = jnp.stack([lax.axis_index("section"), peer // RING, peer % RING]).astype(jnp.int32)
    here, there = inputs[0, 0], cotangent[0, 0]
    e, g = [None] * 8, [None] * 8
    normed, kept, sigma = [None] * 4, (), None

    def run_forward(dz, earlier):
        nonlocal kept, sigma
        *first, normed[dz], qkv, probs, mixed = forward(
            dz, after(ids, earlier), wiring, lengths, norm_gain, w_query, w_key, w_value, e, kept
        )
        kept = (qkv, probs, mixed)
        if dz == 0:
            sigma = first[0]

    def both(value_up, value_down, earlier):
        value_up, value_down = after((value_up, value_down), earlier)
        return moved(value_up, 0, 0, 1), moved(value_down, 0, 0, -1)

    e[0], e[1] = moved(here, 1, 0, 0), moved(here, 1, 1, 0)
    e[6], e[2] = both(e[0], e[0], ())
    g[0], g[1] = moved(after(there, e[0]), -1, 0, 0), moved(after(there, e[0]), -1, 1, 0)
    e[7], e[3] = both(e[1], e[1], ())
    run_forward(0, ())
    e[4] = moved(e[6], 0, 0, 1)
    g[2] = moved(after(g[0], normed[0]), 0, 0, -1)
    g[6] = moved(after(g[0], e[7]), 0, 0, 1)
    run_forward(1, (e[7],))
    e[5] = moved(e[4], 0, 1, 0)
    g[3] = moved(after(g[1], e[3]), 0, 0, -1)
    run_forward(3, ())
    g[7] = moved(after(g[1], (e[4], normed[1])), 0, 0, 1)
    g[4] = moved(after(g[2], normed[3]), 0, 0, -1)
    run_forward(2, ())
    qkv, probs, mixed = kept
    *piece, sent = outward(sigma, mixed, w_out, e)
    dqkv = ()

    def run_back(dz, earlier):
        nonlocal dqkv
        dqkv = (back(dz, after(sigma, earlier), w_out, qkv, probs, g, dqkv),)

    up, down = both(piece[4], piece[5], (g[7], g[3]))
    run_back(0, (sent, g[7], g[3]))
    got_1, got_0 = both(piece[3], piece[6], dqkv)
    g[5] = moved(after(g[4], dqkv), 0, 1, 0)
    run_back(1, ())
    run_back(3, ())
    up, down = after((up, down), dqkv)
    last_0, last_1 = both(add(piece[2], up), add(piece[7], down), ())
    run_back(2, ())
    first_0, first_1 = (piece[0], got_0, last_0), (piece[1], got_1, last_1)
    dqkv, weights = dqkv[0], (w_query, w_key, w_value)
    piece = [None] * 8
    piece[4], piece[5] = inward((4, 5), False, sigma, dqkv, *weights)
    up, down = moved(piece[4], 0, 0, 1), moved(piece[5], 0, 0, -1)
    rest = (3, 6, 7, 2, 0, 1)
    *pieces, dqkv = inward(rest, True, after(sigma, (piece[4], got_0, got_1)), dqkv, *weights)
    for r, value in zip(rest, pieces, strict=True):
        piece[r] = value
    got_1, got_0 = moved(piece[3], 0, 0, 1), moved(piece[6], 0, 0, -1)
    w_query_grad, w_key_grad, w_value_grad, gain_part = weight_grad(
        normed, dqkv, *weights, norm_gain
    )
    first_0, first_1 = after((first_0, first_1), w_query_grad)
    other = moved(add_three(*first_1), 1, 1, 0)
    same = moved(add_three(*first_0), 1, 0, 0)
    up, down = after(up, w_query_grad), after(down, w_query_grad)
    last_1 = moved(add(piece[7], down), 0, 0, -1)
    last_0 = moved(add(piece[2], up), 0, 0, 1)
    w_out_grad = out_grad(after(sent, (got_1, got_0, same, other)), g)
    gain_part = gain_part + moved(after(gain_part, other), 0, 1, 0)
    gain_part = after(gain_part, w_out_grad)
    gain_part = gain_part + paired(gain_part)
    d_out = pick(after(sigma, gain_part), g)
    to_other = end_back(norm_gain, e[1], (piece[1], got_1, last_1))
    to_other = moved(to_other, -1, 1, 0)
    to_same = end_back(norm_gain, e[0], (piece[0], got_0, last_0), d_out)
    final_out = add(same, other)
    gain_grad = gain_part + moved(gain_part, 0, 0, 2)
    input_grad = add(moved(to_same, -1, 0, 0), after(to_other, (gain_grad, final_out)))
    return (
        final_out[None, None],
        input_grad[None, None],
        gain_grad,
        w_query_grad,
        w_key_grad,
        w_value_grad,
        w_out_grad,
    )


def solution(mesh):
    return jax.shard_map(
        per_device,
        mesh=mesh,
        in_specs=(
            P("section", "peer", None, None),
            P(),
            P(),
            P("section", None),
            P("section", None, "peer"),
            P("section", None, "peer"),
            P("section", None, "peer"),
            P("section", "peer", None),
            P("section", "peer", None, None),
        ),
        out_specs=(
            P("section", "peer", None, None),
            P("section", "peer", None, None),
            P("section", None),
            P("section", None, "peer"),
            P("section", None, "peer"),
            P("section", None, "peer"),
            P("section", "peer", None),
        ),
        check_vma=False,
    )
```

```python
import functools
import math

import jax
import jax.numpy as jnp
from jax import lax
from jax.experimental import pallas as pl
from jax.experimental.pallas import tpu as pltpu
from jax.sharding import PartitionSpec as P

HD = 128
TOK = 128
HEADS = 3
LOCAL = HEADS * HD
D = 2560
SECTIONS = 16
RING = 4
SCALE = 1.0 / math.sqrt(HD)
eps = 1e-05

F32 = jnp.float32
BF16 = jnp.bfloat16
VMEM_LIMIT = 24 * 1024 * 1024


def moved(value, by_section, flip, by_ring):
    pairs = []
    for section in range(SECTIONS):
        for side in range(2):
            for place in range(RING):
                source = (section * 2 + side) * RING + place
                target = ((section + by_section) % SECTIONS * 2 + (side ^ flip)) * RING
                pairs.append((source, target + (place + by_ring) % RING))
    return lax.ppermute(value, ("section", "peer"), pairs)


def after(values, earlier):
    return lax.optimization_barrier((values, earlier))[0]


def nt(a, b):
    return lax.dot_general(a, b, (((1,), (1,)), ((), ())), preferred_element_type=F32)


def tn(a, b):
    return lax.dot_general(a, b, (((0,), (0,)), ((), ())), preferred_element_type=F32)


def nn(a, b):
    return jnp.dot(a, b, preferred_element_type=F32)


def load_one(refs, wanted, target, sem):
    for r, ref in enumerate(refs):

        @pl.when(wanted == r)
        def _(ref=ref):
            copy = pltpu.make_async_copy(ref, target, sem)
            copy.start()
            copy.wait()


def absolute(ids, r):
    dz, dx = r // 2, r % 2
    return lax.rem(ids[1] + dx, 2) * RING + lax.rem(ids[2] + dz, RING)


def forward_kernel(dz, ids, wiring, lengths, gain, wq, wk, wv, *rest):
    parts, rest = rest[:2], rest[2:]
    if dz == 0:
        sigma, normed, qkv, probs, mixed, entering, weights, sems = rest
    else:
        normed, qkv, probs, mixed, entering, weights, sems = rest[3:]
    section = ids[0]
    before = lax.rem(section + SECTIONS - 1, SECTIONS)
    w_copies = [
        pltpu.make_async_copy(w.at[0], weights.at[:, pl.ds(c * LOCAL, LOCAL)], sems.at[2 + c])
        for c, w in enumerate((wq, wk, wv))
    ]
    copies = [
        pltpu.make_async_copy(part, entering.at[dx], sems.at[dx]) for dx, part in enumerate(parts)
    ]
    for copy in copies + w_copies:
        copy.start()
    if dz == 0:
        for r in range(8):
            slot = absolute(ids, r)
            found = jnp.int32(0)
            for m in range(8):
                goes_to = wiring[1, section, wiring[0, before, absolute(ids, m)]]
                found = found + jnp.where(goes_to == slot, m, 0)
            sigma[r] = found
    for copy in copies:
        copy.wait()
    gain_row = gain[...].astype(F32)

    def norm_one(i, carry):
        at = pl.ds(pl.multiple_of(i * 32, 32), 32)
        for dx in range(2):
            act = entering[dx, at].astype(F32)
            inv_rms = lax.rsqrt(jnp.mean(act * act, axis=-1, keepdims=True) + eps)
            normed[dx, at] = (act * inv_rms * gain_row).astype(BF16)
        return carry

    lax.fori_loop(0, TOK // 32, norm_one, 0)
    for copy in w_copies:
        copy.wait()
    rows = normed[...].reshape(2 * TOK, D)
    qkv[...] = nn(rows, weights[...]).astype(BF16).reshape(2, TOK, 3 * LOCAL)
    row = lax.broadcasted_iota(jnp.int32, (TOK, TOK), 0)
    col = lax.broadcasted_iota(jnp.int32, (TOK, TOK), 1)
    for dx in range(2):
        seq_len = lengths[before, absolute(ids, 2 * dz + dx)]
        allowed = (row >= col) & (col < seq_len)
        for h in range(HEADS):
            q = qkv[dx, :, h * HD : (h + 1) * HD]
            k = qkv[dx, :, LOCAL + h * HD : LOCAL + (h + 1) * HD]
            v = qkv[dx, :, 2 * LOCAL + h * HD : 2 * LOCAL + (h + 1) * HD]
            scores = jnp.where(allowed, nt(q, k) * SCALE, -1e30)
            exp_scores = jnp.exp(scores - jnp.max(scores, axis=-1, keepdims=True))
            p = exp_scores / jnp.sum(exp_scores, axis=-1, keepdims=True)
            probs[dx, h] = p
            mixed[dx, :, h * HD : (h + 1) * HD] = nn(p.astype(BF16), v).astype(BF16)


ANY = pl.BlockSpec(memory_space=pl.ANY)
SMEM = pl.BlockSpec(memory_space=pltpu.SMEM)
VMEM = pl.BlockSpec(memory_space=pltpu.VMEM)


def params(**more):
    return pltpu.CompilerParams(vmem_limit_bytes=VMEM_LIMIT, **more)


NO_COST = pl.CostEstimate(flops=0, bytes_accessed=0, transcendentals=0)


def forward(dz, ids, wiring, lengths, gain, wq, wk, wv, parts, kept):
    shapes = [
        jax.ShapeDtypeStruct((8, TOK, 3 * LOCAL), BF16),
        jax.ShapeDtypeStruct((8, HEADS, TOK, TOK), F32),
        jax.ShapeDtypeStruct((8, TOK, LOCAL), BF16),
    ]
    specs = [
        pl.BlockSpec((2,) + shape.shape[1:], lambda i, n=len(shape.shape): (dz,) + (0,) * (n - 1))
        for shape in shapes
    ]
    shapes = [jax.ShapeDtypeStruct((2, TOK, D), BF16)] + shapes
    specs = [pl.BlockSpec((2, TOK, D), lambda i: (0, 0, 0))] + specs
    if dz == 0:
        shapes, specs = [jax.ShapeDtypeStruct((8,), jnp.int32)] + shapes, [SMEM] + specs
    return pl.pallas_call(
        functools.partial(forward_kernel, dz),
        grid=(1,),
        out_shape=shapes,
        in_specs=[SMEM] * 3 + [pl.BlockSpec((1, D), lambda i: (0, 0))] + [ANY] * (5 + len(kept)),
        out_specs=specs,
        input_output_aliases={9 + i: 1 + i for i in range(len(kept))},
        scratch_shapes=[
            pltpu.VMEM((2, TOK, D), BF16),
            pltpu.VMEM((D, 3 * LOCAL), BF16),
            pltpu.SemaphoreType.DMA((5,)),
        ],
        compiler_params=params(),
        cost_estimate=NO_COST,
        name="forward",
    )(ids, wiring, lengths, gain, wq, wk, wv, *parts[2 * dz : 2 * dz + 2], *kept)


TILE = 512


def store_pieces(outs, total):
    for r, out in enumerate(outs):
        out[...] = total[r].astype(BF16)


def piece_shapes():
    return (jax.ShapeDtypeStruct((TOK, D), BF16),) * 8


def piece_specs():
    return (pl.BlockSpec((TOK, TILE), lambda n: (0, n)),) * 8


def outward_kernel(sigma, mixed, wo, *rest):
    parts, outs, sent = rest[:8], rest[8:16], rest[16]
    entering, sem = rest[17:]
    tile = pl.program_id(0)

    @pl.when(tile == 0)
    def _():
        for r in range(8):
            sent[r] = mixed[sigma[r]]
        load_one(parts, sigma[0], entering, sem)

    total = nn(sent[...].reshape(8 * TOK, LOCAL), wo[0]).reshape(8, TOK, TILE)
    store_pieces(outs[1:], total[1:])
    residual = entering[:, pl.ds(pl.multiple_of(tile * TILE, TILE), TILE)].astype(F32)
    outs[0][...] = (total[0] + residual).astype(BF16)


def outward(sigma, mixed, wo, parts):
    whole = pl.BlockSpec((8, TOK, LOCAL), lambda n: (0, 0, 0))
    return pl.pallas_call(
        outward_kernel,
        grid=(D // TILE,),
        out_shape=piece_shapes() + (jax.ShapeDtypeStruct((8, TOK, LOCAL), BF16),),
        in_specs=[SMEM, whole, pl.BlockSpec((1, LOCAL, TILE), lambda n: (0, 0, n))] + [ANY] * 8,
        out_specs=piece_specs() + (whole,),
        scratch_shapes=[pltpu.VMEM((TOK, D), BF16), pltpu.SemaphoreType.DMA(())],
        compiler_params=params(),
        cost_estimate=NO_COST,
        name="outward",
    )(sigma, mixed, wo, *parts)


def back_kernel(dz, sigma, wo, qkv, probs, *rest):
    parts = rest[:2]
    dqkv, grads, d_mixed, heads, soft, sems = rest[-6:]
    copies = [
        pltpu.make_async_copy(part, grads.at[dx], sems.at[dx]) for dx, part in enumerate(parts)
    ]
    for dx in range(2):
        m = sigma[2 * dz + dx]
        copies.append(pltpu.make_async_copy(qkv.at[m], heads.at[dx], sems.at[2 + dx]))
        copies.append(pltpu.make_async_copy(probs.at[m], soft.at[dx], sems.at[4 + dx]))
    for copy in copies:
        copy.start()
    for copy in copies:
        copy.wait()
    rows = grads[...].reshape(2 * TOK, D)
    d_mixed[...] = nt(rows, wo[0]).astype(BF16).reshape(2, TOK, LOCAL)
    for dx in range(2):
        for h in range(HEADS):
            cq = slice(h * HD, (h + 1) * HD)
            ck = slice(LOCAL + h * HD, LOCAL + (h + 1) * HD)
            cv = slice(2 * LOCAL + h * HD, 2 * LOCAL + (h + 1) * HD)
            d = d_mixed[dx, :, cq]
            p = soft[dx, h]
            dqkv[dx, :, cv] = tn(p.astype(BF16), d).astype(BF16)
            d_probs = nt(d, heads[dx, :, cv])
            delta = jnp.sum(p * d_probs, axis=-1, keepdims=True)
            d_scores = (p * (d_probs - delta) * SCALE).astype(BF16)
            dqkv[dx, :, cq] = nn(d_scores, heads[dx, :, ck]).astype(BF16)
            dqkv[dx, :, ck] = tn(d_scores, heads[dx, :, cq]).astype(BF16)


def back(dz, sigma, wo, qkv, probs, parts, kept):
    return pl.pallas_call(
        functools.partial(back_kernel, dz),
        grid=(1,),
        out_shape=jax.ShapeDtypeStruct((8, TOK, 3 * LOCAL), BF16),
        in_specs=[SMEM, pl.BlockSpec((1, LOCAL, D), lambda i: (0, 0, 0))] + [ANY] * (4 + len(kept)),
        out_specs=pl.BlockSpec((2, TOK, 3 * LOCAL), lambda i: (dz, 0, 0)),
        input_output_aliases={6 + i: i for i in range(len(kept))},
        scratch_shapes=[
            pltpu.VMEM((2, TOK, D), BF16),
            pltpu.VMEM((2, TOK, LOCAL), BF16),
            pltpu.VMEM((2, TOK, 3 * LOCAL), BF16),
            pltpu.VMEM((2, HEADS, TOK, TOK), F32),
            pltpu.SemaphoreType.DMA((6,)),
        ],
        compiler_params=params(),
        cost_estimate=NO_COST,
        name="back",
    )(sigma, wo, qkv, probs, *parts[2 * dz : 2 * dz + 2], *kept)


def inward_kernel(numbers, sigma, dqkv, wq, wk, wv, *rest):
    outs, (flat, weights) = rest[: len(numbers)], rest[-2:]
    count = len(numbers)

    @pl.when(pl.program_id(0) == 0)
    def _():
        for r in range(8):
            if count == 8:
                flat[sigma[r]] = dqkv[r]
                continue
            for i, number in enumerate(numbers):

                @pl.when(sigma[r] == number)
                def _(r=r, i=i):
                    flat[i] = dqkv[r]

        if len(rest) > count + 2:
            for r in range(8):
                rest[count][sigma[r]] = dqkv[r]

    for c, w in enumerate((wq, wk, wv)):
        weights[:, c * LOCAL : (c + 1) * LOCAL] = w[0]
    total = nt(flat[...].reshape(count * TOK, 3 * LOCAL), weights[...])
    store_pieces(outs, total.reshape(count, TOK, TILE))


def inward(numbers, in_order, sigma, dqkv, wq, wk, wv):
    weight = pl.BlockSpec((1, TILE, LOCAL), lambda n: (0, n, 0))
    whole = pl.BlockSpec((8, TOK, 3 * LOCAL), lambda n: (0, 0, 0))
    count = len(numbers)
    return pl.pallas_call(
        functools.partial(inward_kernel, numbers),
        grid=(D // TILE,),
        out_shape=piece_shapes()[:count]
        + (jax.ShapeDtypeStruct((8, TOK, 3 * LOCAL), BF16),) * in_order,
        in_specs=[SMEM, whole, weight, weight, weight],
        out_specs=piece_specs()[:count] + (whole,) * in_order,
        scratch_shapes=[
            pltpu.VMEM((count, TOK, 3 * LOCAL), BF16),
            pltpu.VMEM((TILE, 3 * LOCAL), BF16),
        ],
        compiler_params=params(),
        cost_estimate=NO_COST,
        name="inward",
    )(sigma, dqkv, wq, wk, wv)


def out_grad_kernel(sent, *rest):
    parts, out, grads = rest[:8], rest[8], rest[9]
    for r, part in enumerate(parts):
        grads[r] = part[...]
    out[0] = tn(
        sent[...].reshape(8 * TOK, LOCAL), grads[...].reshape(8 * TOK, TILE)
    ).astype(BF16)


def out_grad(sent, parts):
    return pl.pallas_call(
        out_grad_kernel,
        grid=(D // TILE,),
        out_shape=jax.ShapeDtypeStruct((1, LOCAL, D), BF16),
        in_specs=[pl.BlockSpec((8, TOK, LOCAL), lambda n: (0, 0, 0))] + list(piece_specs()),
        out_specs=pl.BlockSpec((1, LOCAL, TILE), lambda n: (0, 0, n)),
        scratch_shapes=[pltpu.VMEM((8, TOK, TILE), BF16)],
        compiler_params=params(),
        cost_estimate=NO_COST,
        name="out_grad",
    )(sent, *parts)


def weight_grad_kernel(n0, n1, n2, n3, dqkv, wq, wk, wv, gain, gq, gk, gv, gain_part, rows):
    for dz, n in enumerate((n0, n1, n2, n3)):
        rows[2 * dz : 2 * dz + 2] = n[...]
    flat = dqkv[...].reshape(8 * TOK, 3 * LOCAL)
    total = tn(rows[...].reshape(8 * TOK, TILE), flat)
    along = jnp.zeros((TILE, 1), F32)
    for c, (w, g) in enumerate(((wq, gq), (wk, gk), (wv, gv))):
        part = total[:, c * LOCAL : (c + 1) * LOCAL]
        along = along + jnp.sum(part * w[0].astype(F32), axis=1, keepdims=True)
        g[0] = part.astype(BF16)
    gain_part[...] = along.T / gain[...].astype(F32)


def weight_grad(normed, dqkv, wq, wk, wv, gain):
    tile = pl.BlockSpec((1, TILE, LOCAL), lambda n: (0, n, 0))
    line = pl.BlockSpec((1, TILE), lambda n: (0, n))
    return pl.pallas_call(
        weight_grad_kernel,
        grid=(D // TILE,),
        out_shape=(jax.ShapeDtypeStruct((1, D, LOCAL), BF16),) * 3
        + (jax.ShapeDtypeStruct((1, D), F32),),
        in_specs=[pl.BlockSpec((2, TOK, TILE), lambda n: (0, 0, n))] * 4
        + [pl.BlockSpec((8, TOK, 3 * LOCAL), lambda n: (0, 0, 0))]
        + [tile] * 3
        + [line],
        out_specs=(tile,) * 3 + (line,),
        scratch_shapes=[pltpu.VMEM((8, TOK, TILE), BF16)],
        compiler_params=params(),
        cost_estimate=NO_COST,
        name="weight_grad",
    )(*normed, dqkv, wq, wk, wv, gain)


def sum_kernel(*refs):
    total = refs[0][...].astype(F32)
    for ref in refs[1:-1]:
        total = total + ref[...].astype(F32)
    refs[-1][...] = total.astype(BF16)


def summed(*values):
    return pl.pallas_call(
        sum_kernel,
        grid=(1,),
        out_shape=jax.ShapeDtypeStruct((TOK, D), BF16),
        in_specs=[pl.BlockSpec((TOK, D), lambda n, b=block: (b, 0)) for _, block in values],
        out_specs=pl.BlockSpec((TOK, D), lambda n: (0, 0)),
        compiler_params=params(),
        cost_estimate=NO_COST,
        name="summed",
    )(*[value for value, _ in values])


def add(a, b):
    return summed((a, 0), (b, 0))


def add_three(a, b, c):
    return summed((a, 0), (b, 0), (c, 0))


def pick_kernel(sigma, *refs):
    parts, out, sem = refs[:8], refs[8], refs[9]
    wanted = jnp.int32(0)
    for r in range(8):
        wanted = wanted + jnp.where(sigma[r] == 0, r, 0)
    load_one(parts, wanted, out, sem)


def pick(sigma, parts):
    return pl.pallas_call(
        pick_kernel,
        out_shape=jax.ShapeDtypeStruct((TOK, D), BF16),
        in_specs=[SMEM] + [ANY] * 8,
        out_specs=ANY,
        scratch_shapes=[pltpu.SemaphoreType.DMA(())],
        compiler_params=params(),
        cost_estimate=NO_COST,
        name="pick",
    )(sigma, *parts)


def end_back_kernel(gain, enter, a, b, c, *rest):
    out = rest[-1]
    gain_row = gain[...].astype(F32)
    for i in range(4):
        rows = slice(i * 32, (i + 1) * 32)
        d_normed = a[rows].astype(F32) + b[rows].astype(F32) + c[rows].astype(F32)
        act = enter[rows].astype(F32)
        inv_rms = lax.rsqrt(jnp.mean(act * act, axis=-1, keepdims=True) + eps)
        unit = act * inv_rms
        scaled = d_normed * gain_row
        d_act = inv_rms * (scaled - unit * jnp.mean(scaled * unit, axis=-1, keepdims=True))
        if len(rest) == 2:
            d_act = d_act + rest[0][rows].astype(F32)
        out[rows] = d_act.astype(BF16)


def end_back(gain, enter, pieces, *residual):
    return pl.pallas_call(
        end_back_kernel,
        out_shape=jax.ShapeDtypeStruct((TOK, D), BF16),
        in_specs=[VMEM] * (5 + len(residual)),
        out_specs=VMEM,
        compiler_params=params(),
        cost_estimate=NO_COST,
        name="end_back",
    )(gain, enter, *pieces, *residual)


def paired(value):
    pairs = [(i, i ^ 1) for i in range(SECTIONS * 2 * RING)]
    return lax.ppermute(value, ("section", "peer"), pairs)


def per_device(inputs, wiring, lengths, norm_gain, w_query, w_key, w_value, w_out, cotangent):
    peer = lax.axis_index("peer")
    ids = jnp.stack([lax.axis_index("section"), peer // RING, peer % RING]).astype(jnp.int32)
    here, there = inputs[0, 0], cotangent[0, 0]
    e, g = [None] * 8, [None] * 8
    normed, kept, sigma = [None] * 4, (), None

    def run_forward(dz, earlier):
        nonlocal kept, sigma
        *first, normed[dz], qkv, probs, mixed = forward(
            dz, after(ids, earlier), wiring, lengths, norm_gain, w_query, w_key, w_value, e, kept
        )
        kept = (qkv, probs, mixed)
        if dz == 0:
            sigma = first[0]

    def both(value_up, value_down, earlier):
        value_up, value_down = after((value_up, value_down), earlier)
        return moved(value_up, 0, 0, 1), moved(value_down, 0, 0, -1)

    e[0], e[1] = moved(here, 1, 0, 0), moved(here, 1, 1, 0)
    e[6], e[2] = both(e[0], e[0], ())
    g[0], g[1] = moved(after(there, e[0]), -1, 0, 0), moved(after(there, e[0]), -1, 1, 0)
    e[7], e[3] = both(e[1], e[1], ())
    run_forward(0, ())
    e[4] = moved(e[6], 0, 0, 1)
    g[2] = moved(after(g[0], normed[0]), 0, 0, -1)
    g[6] = moved(after(g[0], e[7]), 0, 0, 1)
    run_forward(1, (e[7],))
    e[5] = moved(e[4], 0, 1, 0)
    g[3] = moved(after(g[1], e[3]), 0, 0, -1)
    run_forward(3, ())
    g[7] = moved(after(g[1], (e[4], normed[1])), 0, 0, 1)
    g[4] = moved(after(g[2], normed[3]), 0, 0, -1)
    run_forward(2, (g[6],))
    qkv, probs, mixed = kept
    *piece, sent = outward(sigma, mixed, w_out, e)
    dqkv = ()

    def run_back(dz, earlier):
        nonlocal dqkv
        dqkv = (back(dz, after(sigma, earlier), w_out, qkv, probs, g, dqkv),)

    up, down = both(piece[4], piece[5], (g[7], g[3]))
    run_back(0, (sent, g[7], g[3]))
    got_1, got_0 = both(piece[3], piece[6], dqkv)
    g[5] = moved(after(g[4], dqkv), 0, 1, 0)
    run_back(1, ())
    run_back(3, ())
    up, down = after((up, down), dqkv)
    last_0, last_1 = both(add(piece[2], up), add(piece[7], down), ())
    run_back(2, ())
    first_0, first_1 = (piece[0], got_0, last_0), (piece[1], got_1, last_1)
    dqkv, weights = dqkv[0], (w_query, w_key, w_value)
    piece = [None] * 8
    piece[4], piece[5] = inward((4, 5), False, sigma, dqkv, *weights)
    up, down = moved(piece[4], 0, 0, 1), moved(piece[5], 0, 0, -1)
    rest = (3, 6, 7, 2, 0, 1)
    *pieces, dqkv = inward(rest, True, after(sigma, (piece[4], got_0, got_1)), dqkv, *weights)
    for r, value in zip(rest, pieces, strict=True):
        piece[r] = value
    got_1, got_0 = moved(piece[3], 0, 0, 1), moved(piece[6], 0, 0, -1)
    w_query_grad, w_key_grad, w_value_grad, gain_part = weight_grad(
        normed, dqkv, *weights, norm_gain
    )
    first_0, first_1 = after((first_0, first_1), w_query_grad)
    other = moved(add_three(*first_1), 1, 1, 0)
    same = moved(add_three(*first_0), 1, 0, 0)
    up, down = after(up, w_query_grad), after(down, w_query_grad)
    last_1 = moved(add(piece[7], down), 0, 0, -1)
    last_0 = moved(add(piece[2], up), 0, 0, 1)
    w_out_grad = out_grad(after(sent, (got_1, got_0, same, other)), g)
    gain_part = gain_part + moved(after(gain_part, other), 0, 1, 0)
    gain_part = after(gain_part, w_out_grad)
    gain_part = gain_part + paired(gain_part)
    d_out = pick(after(sigma, gain_part), g)
    to_other = end_back(norm_gain, e[1], (piece[1], got_1, last_1))
    to_other = moved(to_other, -1, 1, 0)
    to_same = end_back(norm_gain, e[0], (piece[0], got_0, last_0), d_out)
    final_out = add(same, other)
    gain_grad = gain_part + moved(gain_part, 0, 0, 2)
    input_grad = add(moved(to_same, -1, 0, 0), after(to_other, (gain_grad, final_out)))
    return (
        final_out[None, None],
        input_grad[None, None],
        gain_grad,
        w_query_grad,
        w_key_grad,
        w_value_grad,
        w_out_grad,
    )


def solution(mesh):
    return jax.shard_map(
        per_device,
        mesh=mesh,
        in_specs=(
            P("section", "peer", None, None),
            P(),
            P(),
            P("section", None),
            P("section", None, "peer"),
            P("section", None, "peer"),
            P("section", None, "peer"),
            P("section", "peer", None),
            P("section", "peer", None, None),
        ),
        out_specs=(
            P("section", "peer", None, None),
            P("section", "peer", None, None),
            P("section", None),
            P("section", None, "peer"),
            P("section", None, "peer"),
            P("section", None, "peer"),
            P("section", "peer", None),
        ),
        check_vma=False,
    )
```

```python
import functools
import math

import jax
import jax.numpy as jnp
from jax import lax
from jax.experimental import pallas as pl
from jax.experimental.pallas import tpu as pltpu
from jax.sharding import PartitionSpec as P

HD = 128
TOK = 128
HEADS = 3
LOCAL = HEADS * HD
D = 2560
SECTIONS = 16
RING = 4
SCALE = 1.0 / math.sqrt(HD)
eps = 1e-05

F32 = jnp.float32
BF16 = jnp.bfloat16
VMEM_LIMIT = 24 * 1024 * 1024


def moved(value, by_section, flip, by_ring):
    pairs = []
    for section in range(SECTIONS):
        for side in range(2):
            for place in range(RING):
                source = (section * 2 + side) * RING + place
                target = ((section + by_section) % SECTIONS * 2 + (side ^ flip)) * RING
                pairs.append((source, target + (place + by_ring) % RING))
    return lax.ppermute(value, ("section", "peer"), pairs)


def after(values, earlier):
    return lax.optimization_barrier((values, earlier))[0]


def nt(a, b):
    return lax.dot_general(a, b, (((1,), (1,)), ((), ())), preferred_element_type=F32)


def tn(a, b):
    return lax.dot_general(a, b, (((0,), (0,)), ((), ())), preferred_element_type=F32)


def nn(a, b):
    return jnp.dot(a, b, preferred_element_type=F32)


def load_one(refs, wanted, target, sem):
    for r, ref in enumerate(refs):

        @pl.when(wanted == r)
        def _(ref=ref):
            copy = pltpu.make_async_copy(ref, target, sem)
            copy.start()
            copy.wait()


def absolute(ids, r):
    dz, dx = r // 2, r % 2
    return lax.rem(ids[1] + dx, 2) * RING + lax.rem(ids[2] + dz, RING)


def forward_kernel(dz, ids, wiring, lengths, gain, wq, wk, wv, *rest):
    parts, rest = rest[:2], rest[2:]
    if dz == 0:
        sigma, normed, qkv, probs, mixed, entering, weights, sems = rest
    else:
        normed, qkv, probs, mixed, entering, weights, sems = rest[3:]
    section = ids[0]
    before = lax.rem(section + SECTIONS - 1, SECTIONS)
    w_copies = [
        pltpu.make_async_copy(w.at[0], weights.at[:, pl.ds(c * LOCAL, LOCAL)], sems.at[2 + c])
        for c, w in enumerate((wq, wk, wv))
    ]
    copies = [
        pltpu.make_async_copy(part, entering.at[dx], sems.at[dx]) for dx, part in enumerate(parts)
    ]
    for copy in copies + w_copies:
        copy.start()
    if dz == 0:
        for r in range(8):
            slot = absolute(ids, r)
            found = jnp.int32(0)
            for m in range(8):
                goes_to = wiring[1, section, wiring[0, before, absolute(ids, m)]]
                found = found + jnp.where(goes_to == slot, m, 0)
            sigma[r] = found
    for copy in copies:
        copy.wait()
    gain_row = gain[...].astype(F32)

    def norm_one(i, carry):
        at = pl.ds(pl.multiple_of(i * 32, 32), 32)
        for dx in range(2):
            act = entering[dx, at].astype(F32)
            inv_rms = lax.rsqrt(jnp.mean(act * act, axis=-1, keepdims=True) + eps)
            normed[dx, at] = (act * inv_rms * gain_row).astype(BF16)
        return carry

    lax.fori_loop(0, TOK // 32, norm_one, 0)
    for copy in w_copies:
        copy.wait()
    rows = normed[...].reshape(2 * TOK, D)
    qkv[...] = nn(rows, weights[...]).astype(BF16).reshape(2, TOK, 3 * LOCAL)
    row = lax.broadcasted_iota(jnp.int32, (TOK, TOK), 0)
    col = lax.broadcasted_iota(jnp.int32, (TOK, TOK), 1)
    for dx in range(2):
        seq_len = lengths[before, absolute(ids, 2 * dz + dx)]
        allowed = (row >= col) & (col < seq_len)
        for h in range(HEADS):
            q = qkv[dx, :, h * HD : (h + 1) * HD]
            k = qkv[dx, :, LOCAL + h * HD : LOCAL + (h + 1) * HD]
            v = qkv[dx, :, 2 * LOCAL + h * HD : 2 * LOCAL + (h + 1) * HD]
            scores = jnp.where(allowed, nt(q, k) * SCALE, -1e30)
            exp_scores = jnp.exp(scores - jnp.max(scores, axis=-1, keepdims=True))
            p = exp_scores / jnp.sum(exp_scores, axis=-1, keepdims=True)
            probs[dx, h] = p
            mixed[dx, :, h * HD : (h + 1) * HD] = nn(p.astype(BF16), v).astype(BF16)


ANY = pl.BlockSpec(memory_space=pl.ANY)
SMEM = pl.BlockSpec(memory_space=pltpu.SMEM)
VMEM = pl.BlockSpec(memory_space=pltpu.VMEM)


def params(**more):
    return pltpu.CompilerParams(vmem_limit_bytes=VMEM_LIMIT, **more)


NO_COST = pl.CostEstimate(flops=0, bytes_accessed=0, transcendentals=0)


def forward(dz, ids, wiring, lengths, gain, wq, wk, wv, parts, kept):
    shapes = [
        jax.ShapeDtypeStruct((8, TOK, 3 * LOCAL), BF16),
        jax.ShapeDtypeStruct((8, HEADS, TOK, TOK), F32),
        jax.ShapeDtypeStruct((8, TOK, LOCAL), BF16),
    ]
    specs = [
        pl.BlockSpec((2,) + shape.shape[1:], lambda i, n=len(shape.shape): (dz,) + (0,) * (n - 1))
        for shape in shapes
    ]
    shapes = [jax.ShapeDtypeStruct((2, TOK, D), BF16)] + shapes
    specs = [pl.BlockSpec((2, TOK, D), lambda i: (0, 0, 0))] + specs
    if dz == 0:
        shapes, specs = [jax.ShapeDtypeStruct((8,), jnp.int32)] + shapes, [SMEM] + specs
    return pl.pallas_call(
        functools.partial(forward_kernel, dz),
        grid=(1,),
        out_shape=shapes,
        in_specs=[SMEM] * 3 + [pl.BlockSpec((1, D), lambda i: (0, 0))] + [ANY] * (5 + len(kept)),
        out_specs=specs,
        input_output_aliases={9 + i: 1 + i for i in range(len(kept))},
        scratch_shapes=[
            pltpu.VMEM((2, TOK, D), BF16),
            pltpu.VMEM((D, 3 * LOCAL), BF16),
            pltpu.SemaphoreType.DMA((5,)),
        ],
        compiler_params=params(),
        cost_estimate=NO_COST,
        name="forward",
    )(ids, wiring, lengths, gain, wq, wk, wv, *parts[2 * dz : 2 * dz + 2], *kept)


TILE = 512


def store_pieces(outs, total):
    for r, out in enumerate(outs):
        out[...] = total[r].astype(BF16)


def piece_shapes():
    return (jax.ShapeDtypeStruct((TOK, D), BF16),) * 8


def piece_specs():
    return (pl.BlockSpec((TOK, TILE), lambda n: (0, n)),) * 8


def outward_kernel(sigma, mixed, wo, *rest):
    parts, outs, sent = rest[:8], rest[8:16], rest[16]
    entering, sem = rest[17:]
    tile = pl.program_id(0)

    @pl.when(tile == 0)
    def _():
        for r in range(8):
            sent[r] = mixed[sigma[r]]
        load_one(parts, sigma[0], entering, sem)

    total = nn(sent[...].reshape(8 * TOK, LOCAL), wo[0]).reshape(8, TOK, TILE)
    store_pieces(outs[1:], total[1:])
    residual = entering[:, pl.ds(pl.multiple_of(tile * TILE, TILE), TILE)].astype(F32)
    outs[0][...] = (total[0] + residual).astype(BF16)


def outward(sigma, mixed, wo, parts):
    whole = pl.BlockSpec((8, TOK, LOCAL), lambda n: (0, 0, 0))
    return pl.pallas_call(
        outward_kernel,
        grid=(D // TILE,),
        out_shape=piece_shapes() + (jax.ShapeDtypeStruct((8, TOK, LOCAL), BF16),),
        in_specs=[SMEM, whole, pl.BlockSpec((1, LOCAL, TILE), lambda n: (0, 0, n))] + [ANY] * 8,
        out_specs=piece_specs() + (whole,),
        scratch_shapes=[pltpu.VMEM((TOK, D), BF16), pltpu.SemaphoreType.DMA(())],
        compiler_params=params(),
        cost_estimate=NO_COST,
        name="outward",
    )(sigma, mixed, wo, *parts)


def back_kernel(dz, sigma, wo, qkv, probs, *rest):
    parts = rest[:2]
    dqkv, grads, d_mixed, heads, soft, sems = rest[-6:]
    copies = [
        pltpu.make_async_copy(part, grads.at[dx], sems.at[dx]) for dx, part in enumerate(parts)
    ]
    for dx in range(2):
        m = sigma[2 * dz + dx]
        copies.append(pltpu.make_async_copy(qkv.at[m], heads.at[dx], sems.at[2 + dx]))
        copies.append(pltpu.make_async_copy(probs.at[m], soft.at[dx], sems.at[4 + dx]))
    for copy in copies:
        copy.start()
    for copy in copies:
        copy.wait()
    rows = grads[...].reshape(2 * TOK, D)
    d_mixed[...] = nt(rows, wo[0]).astype(BF16).reshape(2, TOK, LOCAL)
    for dx in range(2):
        for h in range(HEADS):
            cq = slice(h * HD, (h + 1) * HD)
            ck = slice(LOCAL + h * HD, LOCAL + (h + 1) * HD)
            cv = slice(2 * LOCAL + h * HD, 2 * LOCAL + (h + 1) * HD)
            d = d_mixed[dx, :, cq]
            p = soft[dx, h]
            dqkv[dx, :, cv] = tn(p.astype(BF16), d).astype(BF16)
            d_probs = nt(d, heads[dx, :, cv])
            delta = jnp.sum(p * d_probs, axis=-1, keepdims=True)
            d_scores = (p * (d_probs - delta) * SCALE).astype(BF16)
            dqkv[dx, :, cq] = nn(d_scores, heads[dx, :, ck]).astype(BF16)
            dqkv[dx, :, ck] = tn(d_scores, heads[dx, :, cq]).astype(BF16)


def back(dz, sigma, wo, qkv, probs, parts, kept):
    return pl.pallas_call(
        functools.partial(back_kernel, dz),
        grid=(1,),
        out_shape=jax.ShapeDtypeStruct((8, TOK, 3 * LOCAL), BF16),
        in_specs=[SMEM, pl.BlockSpec((1, LOCAL, D), lambda i: (0, 0, 0))] + [ANY] * (4 + len(kept)),
        out_specs=pl.BlockSpec((2, TOK, 3 * LOCAL), lambda i: (dz, 0, 0)),
        input_output_aliases={6 + i: i for i in range(len(kept))},
        scratch_shapes=[
            pltpu.VMEM((2, TOK, D), BF16),
            pltpu.VMEM((2, TOK, LOCAL), BF16),
            pltpu.VMEM((2, TOK, 3 * LOCAL), BF16),
            pltpu.VMEM((2, HEADS, TOK, TOK), F32),
            pltpu.SemaphoreType.DMA((6,)),
        ],
        compiler_params=params(),
        cost_estimate=NO_COST,
        name="back",
    )(sigma, wo, qkv, probs, *parts[2 * dz : 2 * dz + 2], *kept)


def inward_kernel(numbers, sigma, dqkv, wq, wk, wv, *rest):
    outs, (flat, weights) = rest[: len(numbers)], rest[-2:]
    count = len(numbers)

    @pl.when(pl.program_id(0) == 0)
    def _():
        for r in range(8):
            if count == 8:
                flat[sigma[r]] = dqkv[r]
                continue
            for i, number in enumerate(numbers):

                @pl.when(sigma[r] == number)
                def _(r=r, i=i):
                    flat[i] = dqkv[r]

        if len(rest) > count + 2:
            for r in range(8):
                rest[count][sigma[r]] = dqkv[r]

    for c, w in enumerate((wq, wk, wv)):
        weights[:, c * LOCAL : (c + 1) * LOCAL] = w[0]
    total = nt(flat[...].reshape(count * TOK, 3 * LOCAL), weights[...])
    store_pieces(outs, total.reshape(count, TOK, TILE))


def inward(numbers, in_order, sigma, dqkv, wq, wk, wv):
    weight = pl.BlockSpec((1, TILE, LOCAL), lambda n: (0, n, 0))
    whole = pl.BlockSpec((8, TOK, 3 * LOCAL), lambda n: (0, 0, 0))
    count = len(numbers)
    return pl.pallas_call(
        functools.partial(inward_kernel, numbers),
        grid=(D // TILE,),
        out_shape=piece_shapes()[:count]
        + (jax.ShapeDtypeStruct((8, TOK, 3 * LOCAL), BF16),) * in_order,
        in_specs=[SMEM, whole, weight, weight, weight],
        out_specs=piece_specs()[:count] + (whole,) * in_order,
        scratch_shapes=[
            pltpu.VMEM((count, TOK, 3 * LOCAL), BF16),
            pltpu.VMEM((TILE, 3 * LOCAL), BF16),
        ],
        compiler_params=params(),
        cost_estimate=NO_COST,
        name="inward",
    )(sigma, dqkv, wq, wk, wv)


def out_grad_kernel(sent, *rest):
    parts, out, grads = rest[:8], rest[8], rest[9]
    for r, part in enumerate(parts):
        grads[r] = part[...]
    out[0] = tn(
        sent[...].reshape(8 * TOK, LOCAL), grads[...].reshape(8 * TOK, TILE)
    ).astype(BF16)


def out_grad(sent, parts):
    return pl.pallas_call(
        out_grad_kernel,
        grid=(D // TILE,),
        out_shape=jax.ShapeDtypeStruct((1, LOCAL, D), BF16),
        in_specs=[pl.BlockSpec((8, TOK, LOCAL), lambda n: (0, 0, 0))] + list(piece_specs()),
        out_specs=pl.BlockSpec((1, LOCAL, TILE), lambda n: (0, 0, n)),
        scratch_shapes=[pltpu.VMEM((8, TOK, TILE), BF16)],
        compiler_params=params(),
        cost_estimate=NO_COST,
        name="out_grad",
    )(sent, *parts)


def weight_grad_kernel(n0, n1, n2, n3, dqkv, wq, wk, wv, gain, gq, gk, gv, gain_part, rows):
    for dz, n in enumerate((n0, n1, n2, n3)):
        rows[2 * dz : 2 * dz + 2] = n[...]
    flat = dqkv[...].reshape(8 * TOK, 3 * LOCAL)
    total = tn(rows[...].reshape(8 * TOK, TILE), flat)
    along = jnp.zeros((TILE, 1), F32)
    for c, (w, g) in enumerate(((wq, gq), (wk, gk), (wv, gv))):
        part = total[:, c * LOCAL : (c + 1) * LOCAL]
        along = along + jnp.sum(part * w[0].astype(F32), axis=1, keepdims=True)
        g[0] = part.astype(BF16)
    gain_part[...] = along.T / gain[...].astype(F32)


def weight_grad(normed, dqkv, wq, wk, wv, gain):
    tile = pl.BlockSpec((1, TILE, LOCAL), lambda n: (0, n, 0))
    line = pl.BlockSpec((1, TILE), lambda n: (0, n))
    return pl.pallas_call(
        weight_grad_kernel,
        grid=(D // TILE,),
        out_shape=(jax.ShapeDtypeStruct((1, D, LOCAL), BF16),) * 3
        + (jax.ShapeDtypeStruct((1, D), F32),),
        in_specs=[pl.BlockSpec((2, TOK, TILE), lambda n: (0, 0, n))] * 4
        + [pl.BlockSpec((8, TOK, 3 * LOCAL), lambda n: (0, 0, 0))]
        + [tile] * 3
        + [line],
        out_specs=(tile,) * 3 + (line,),
        scratch_shapes=[pltpu.VMEM((8, TOK, TILE), BF16)],
        compiler_params=params(),
        cost_estimate=NO_COST,
        name="weight_grad",
    )(*normed, dqkv, wq, wk, wv, gain)


def sum_kernel(*refs):
    total = refs[0][...].astype(F32)
    for ref in refs[1:-1]:
        total = total + ref[...].astype(F32)
    refs[-1][...] = total.astype(BF16)


def summed(*values):
    return pl.pallas_call(
        sum_kernel,
        grid=(1,),
        out_shape=jax.ShapeDtypeStruct((TOK, D), BF16),
        in_specs=[pl.BlockSpec((TOK, D), lambda n, b=block: (b, 0)) for _, block in values],
        out_specs=pl.BlockSpec((TOK, D), lambda n: (0, 0)),
        compiler_params=params(),
        cost_estimate=NO_COST,
        name="summed",
    )(*[value for value, _ in values])


def add(a, b):
    return summed((a, 0), (b, 0))


def add_three(a, b, c):
    return summed((a, 0), (b, 0), (c, 0))


def pick_kernel(sigma, *refs):
    parts, out, sem = refs[:8], refs[8], refs[9]
    wanted = jnp.int32(0)
    for r in range(8):
        wanted = wanted + jnp.where(sigma[r] == 0, r, 0)
    load_one(parts, wanted, out, sem)


def pick(sigma, parts):
    return pl.pallas_call(
        pick_kernel,
        out_shape=jax.ShapeDtypeStruct((TOK, D), BF16),
        in_specs=[SMEM] + [ANY] * 8,
        out_specs=ANY,
        scratch_shapes=[pltpu.SemaphoreType.DMA(())],
        compiler_params=params(),
        cost_estimate=NO_COST,
        name="pick",
    )(sigma, *parts)


def end_back_kernel(gain, enter, a, b, c, *rest):
    out = rest[-1]
    gain_row = gain[...].astype(F32)
    for i in range(4):
        rows = slice(i * 32, (i + 1) * 32)
        d_normed = a[rows].astype(F32) + b[rows].astype(F32) + c[rows].astype(F32)
        act = enter[rows].astype(F32)
        inv_rms = lax.rsqrt(jnp.mean(act * act, axis=-1, keepdims=True) + eps)
        unit = act * inv_rms
        scaled = d_normed * gain_row
        d_act = inv_rms * (scaled - unit * jnp.mean(scaled * unit, axis=-1, keepdims=True))
        if len(rest) == 2:
            d_act = d_act + rest[0][rows].astype(F32)
        out[rows] = d_act.astype(BF16)


def end_back(gain, enter, pieces, *residual):
    return pl.pallas_call(
        end_back_kernel,
        out_shape=jax.ShapeDtypeStruct((TOK, D), BF16),
        in_specs=[VMEM] * (5 + len(residual)),
        out_specs=VMEM,
        compiler_params=params(),
        cost_estimate=NO_COST,
        name="end_back",
    )(gain, enter, *pieces, *residual)


def paired(value):
    pairs = [(i, i ^ 1) for i in range(SECTIONS * 2 * RING)]
    return lax.ppermute(value, ("section", "peer"), pairs)


def per_device(inputs, wiring, lengths, norm_gain, w_query, w_key, w_value, w_out, cotangent):
    peer = lax.axis_index("peer")
    ids = jnp.stack([lax.axis_index("section"), peer // RING, peer % RING]).astype(jnp.int32)
    here, there = inputs[0, 0], cotangent[0, 0]
    e, g = [None] * 8, [None] * 8
    normed, kept, sigma = [None] * 4, (), None

    def run_forward(dz, earlier):
        nonlocal kept, sigma
        *first, normed[dz], qkv, probs, mixed = forward(
            dz, after(ids, earlier), wiring, lengths, norm_gain, w_query, w_key, w_value, e, kept
        )
        kept = (qkv, probs, mixed)
        if dz == 0:
            sigma = first[0]

    def both(value_up, value_down, earlier):
        value_up, value_down = after((value_up, value_down), earlier)
        return moved(value_up, 0, 0, 1), moved(value_down, 0, 0, -1)

    e[0], e[1] = moved(here, 1, 0, 0), moved(here, 1, 1, 0)
    e[6], e[2] = both(e[0], e[0], ())
    g[0], g[1] = moved(after(there, e[0]), -1, 0, 0), moved(after(there, e[0]), -1, 1, 0)
    e[7], e[3] = both(e[1], e[1], ())
    run_forward(0, ())
    e[4] = moved(e[6], 0, 0, 1)
    g[2] = moved(after(g[0], normed[0]), 0, 0, -1)
    g[6] = moved(after(g[0], e[7]), 0, 0, 1)
    run_forward(1, (e[7],))
    e[5] = moved(e[4], 0, 1, 0)
    g[3] = moved(after(g[1], e[3]), 0, 0, -1)
    run_forward(3, ())
    g[7] = moved(after(g[1], (e[4], normed[1])), 0, 0, 1)
    g[4] = moved(after(g[2], normed[3]), 0, 0, -1)
    run_forward(2, (g[6],))
    qkv, probs, mixed = kept
    *piece, sent = outward(sigma, mixed, w_out, e)
    dqkv = ()

    def run_back(dz, earlier):
        nonlocal dqkv
        dqkv = (back(dz, after(sigma, earlier), w_out, qkv, probs, g, dqkv),)

    up, down = both(piece[4], piece[5], (g[7], g[3]))
    run_back(0, (sent, g[7], g[3]))
    got_1, got_0 = both(piece[3], piece[6], dqkv)
    g[5] = moved(after(g[4], dqkv), 0, 1, 0)
    run_back(1, ())
    run_back(3, ())
    up, down = after((up, down), dqkv)
    last_0, last_1 = both(add(piece[2], up), add(piece[7], down), ())
    run_back(2, ())
    first_0, first_1 = (piece[0], got_0, last_0), (piece[1], got_1, last_1)
    dqkv, weights = dqkv[0], (w_query, w_key, w_value)
    piece = [None] * 8
    piece[4], piece[5] = inward((4, 5), False, sigma, dqkv, *weights)
    up, down = moved(piece[4], 0, 0, 1), moved(piece[5], 0, 0, -1)
    rest = (3, 6, 7, 2, 0, 1)
    *pieces, dqkv = inward(rest, True, after(sigma, (piece[4], got_0, got_1)), dqkv, *weights)
    for r, value in zip(rest, pieces, strict=True):
        piece[r] = value
    got_1, got_0 = moved(piece[3], 0, 0, 1), moved(piece[6], 0, 0, -1)
    w_query_grad, w_key_grad, w_value_grad, gain_part = weight_grad(
        normed, dqkv, *weights, norm_gain
    )
    first_0, first_1 = after((first_0, first_1), w_query_grad)
    other = moved(add_three(*first_1), 1, 1, 0)
    up, down = after(up, w_query_grad), after(down, w_query_grad)
    last_1 = moved(add(piece[7], down), 0, 0, -1)
    last_0 = moved(add(piece[2], up), 0, 0, 1)
    same = moved(after(add_three(*first_0), last_1), 1, 0, 0)
    w_out_grad = out_grad(after(sent, (got_1, got_0, other)), g)
    gain_part = gain_part + moved(after(gain_part, other), 0, 1, 0)
    gain_part = after(gain_part, w_out_grad)
    gain_part = gain_part + paired(gain_part)
    d_out = pick(after(sigma, gain_part), g)
    to_other = end_back(norm_gain, e[1], (piece[1], got_1, last_1))
    to_other = moved(to_other, -1, 1, 0)
    to_same = end_back(norm_gain, e[0], (piece[0], got_0, last_0), d_out)
    final_out = add(same, other)
    gain_grad = gain_part + moved(gain_part, 0, 0, 2)
    input_grad = add(moved(to_same, -1, 0, 0), after(to_other, (gain_grad, final_out)))
    return (
        final_out[None, None],
        input_grad[None, None],
        gain_grad,
        w_query_grad,
        w_key_grad,
        w_value_grad,
        w_out_grad,
    )


def solution(mesh):
    return jax.shard_map(
        per_device,
        mesh=mesh,
        in_specs=(
            P("section", "peer", None, None),
            P(),
            P(),
            P("section", None),
            P("section", None, "peer"),
            P("section", None, "peer"),
            P("section", None, "peer"),
            P("section", "peer", None),
            P("section", "peer", None, None),
        ),
        out_specs=(
            P("section", "peer", None, None),
            P("section", "peer", None, None),
            P("section", None),
            P("section", None, "peer"),
            P("section", None, "peer"),
            P("section", None, "peer"),
            P("section", "peer", None),
        ),
        check_vma=False,
    )
```
